256 devices in a mesh: rows: 4 (over y), vocab: 64 (over z, x, core).
Axes of the slice: x: 4, y: 4, z: 8, core: 2. Of those that a mesh axis runs over, the one named last changes fastest.
Arguments:
- hidden: bfloat16 [2048, 7168], P('vocab', 'rows'), may hold values from -50 to 50
- head_weight: bfloat16 [7168, 65536], P('rows', 'vocab'), may hold values from -2 to 2
- draft_probs: float32 [2048, 65536], P(('rows', 'vocab')), may hold values from 0 to 1, as said below
- draft_ids: int32 [2048, 1], P('rows'), may hold values from 0 to 65535
Outputs:
- residual: float32 [2048, 65536], P('rows', 'vocab')
- accept_ratio: float32 [2048], P('rows')
The draws below stay inside these ranges and needn't reach their ends.
Inputs may be any that keep to these rules, and one draw needn't show every extreme that they name: Each row of draft_probs sums to one, up to rounding.
All inputs are finite; a program needn't handle non-finite values.
Results may differ from the reference program's by a relative error of at most 0.0012.
Values may be sent and summed in bfloat16 or wider, within the bound.
A program may use at most 128 MiB of HBM per device.

```python
import math
import jax
import jax.numpy as jnp

D = 7168
TOKENS = 2048
VOCAB = 65536


mixing_share = 0.02


def column_scales(key):
    values = jax.random.uniform(jax.random.fold_in(key, 700), (1, VOCAB), jnp.float32, math.log(0.5), math.log(2.0))
    return jnp.exp(values)


def drafted_tokens(key):
    first_key, second_key = jax.random.split(jax.random.fold_in(key, 600))
    token_ids = jax.random.randint(first_key, (TOKENS,), 0, VOCAB, jnp.int32)
    places = jax.random.randint(second_key, (2,), 0, TOKENS // 2, jnp.int32)
    token_ids = token_ids.at[places[0]].set(0).at[places[1] + TOKENS // 2].set(VOCAB - 1)
    return token_ids


def draw_draft_ids(key, part):
    token_ids = drafted_tokens(key)
    return token_ids[:, None]


def draw_head_weight(key, part):
    scales = column_scales(key)
    key = jax.random.fold_in(key, 2)
    first_key = jax.random.fold_in(key, 0)
    base = jnp.clip(jax.random.normal(first_key, (D, VOCAB), jnp.float32), -5.0, 5.0)
    matrix = base * scales / math.sqrt(D)
    return matrix.astype(jnp.bfloat16)


def draw_hidden(key, part):
    scales = column_scales(key)
    token_ids = drafted_tokens(key)
    head = draw_head_weight(key, part)
    picked_columns = jnp.take(head, token_ids, axis=1).astype(jnp.float32)
    picked_scale = jnp.take(scales[0], token_ids)
    limit = 10.0 / math.sqrt(D)
    direction = jnp.clip(picked_columns.T / (picked_scale[:, None] * picked_scale[:, None]), -limit, limit)
    key = jax.random.fold_in(key, 1)
    first_key, second_key, third_key = jax.random.split(key, 3)
    base = jnp.clip(jax.random.normal(first_key, (TOKENS, D), jnp.float32), -5.0, 5.0)
    row_scale = jnp.exp(jax.random.uniform(second_key, (TOKENS, 1), jnp.float32, math.log(2.0), math.log(8.0)))
    reach = math.sqrt(2.0 * math.log(VOCAB))
    lift = row_scale * 1.16 * reach * jax.random.uniform(third_key, (TOKENS, 1), jnp.float32, 0.75, 1.3)
    field = base * row_scale + lift * direction
    return field.astype(jnp.bfloat16)


def draw_draft_probs(key, part):
    hidden = draw_hidden(key, part)
    head = draw_head_weight(key, part)
    logits = jnp.dot(hidden, head, preferred_element_type=jnp.float32)
    key = jax.random.fold_in(key, 4)
    first_key, second_key = jax.random.split(key)
    noise = jnp.clip(jax.random.normal(first_key, (TOKENS, VOCAB), jnp.float32), -5.0, 5.0)
    spread = jnp.exp(jax.random.uniform(second_key, (TOKENS, 1), jnp.float32, math.log(0.02), math.log(1.5)))
    shifted = logits + spread * noise
    shifted = shifted - jnp.max(shifted, axis=1, keepdims=True)
    weights = jnp.exp(shifted)
    smooth = weights / jnp.sum(weights, axis=1, keepdims=True)
    return (1.0 - mixing_share) * smooth + mixing_share / VOCAB


def setup_inputs(seed: int = 0) -> dict:
    keys = jax.random.split(jax.random.key(seed), 5)
    return {
        "hidden": draw_hidden(jax.random.fold_in(keys[4], 71), 0),
        "head_weight": draw_head_weight(jax.random.fold_in(keys[4], 71), 0),
        "draft_probs": draw_draft_probs(jax.random.fold_in(keys[4], 71), 0),
        "draft_ids": draw_draft_ids(jax.random.fold_in(keys[4], 71), 0),
    }


mass_floor = 0.05


def reference(hidden, head_weight, draft_probs, draft_ids):
    logits = jnp.dot(hidden, head_weight, preferred_element_type=jnp.float32)
    top = jnp.max(logits, axis=1, keepdims=True)
    weights = jnp.exp(logits - top)
    total = jnp.sum(weights, axis=1, keepdims=True)
    target = weights / total
    picked_weight = jnp.take_along_axis(weights, draft_ids.astype(jnp.int32), axis=1)
    picked_draft = jnp.take_along_axis(draft_probs, draft_ids.astype(jnp.int32), axis=1)
    accept_ratio = jnp.minimum(jnp.float32(1.0), (picked_weight / total) / picked_draft)[:, 0]
    excess = jnp.maximum(target - draft_probs, jnp.float32(0.0))
    mass = jnp.sum(excess, axis=1, keepdims=True)
    residual = excess / jnp.maximum(mass, mass_floor)
    return residual, accept_ratio
```

```python
import functools

import jax
import jax.numpy as jnp
from jax import lax
from jax.experimental import pallas as pl
from jax.experimental.pallas import tpu as pltpu
from jax.sharding import PartitionSpec as P

MESH = pl.DeviceIdType.MESH
F32 = jnp.float32
mass_floor = 0.05

NY, NZ, NX, NC = 4, 8, 4, 2
NV = NZ * NX * NC
SHARD = 16
HALF_K = 896


def rows_to_lanes(ref):
    return jnp.transpose(ref[...], (1, 0))


def lanes_to_rows(row):
    return jnp.transpose(jnp.broadcast_to(row, (128, row.shape[1])), (1, 0))


def tile8(block):
    return jnp.concatenate([block] * 8, axis=1)


def fold8(block):
    total = block[:, 0:128]
    for i in range(1, 8):
        total = total + block[:, 128 * i : 128 * (i + 1)]
    return total


def kernel(
    hid, w_hbm, draft_hbm, ids_ref, out_hbm, acc_ref,
    G, W, part, leg, fin, dr, E, idc, colm, cola, colb, colc, S1, S2,
    ag_send, ag_recv, y_send, y_recv, st_send, st_recv, dr_send, dr_recv, loc,
):
    r = lax.axis_index("rows")
    v = lax.axis_index("vocab")
    z = v // (NX * NC)
    x = (v // NC) % NX
    c = v % NC
    xc = v % (NX * NC)

    def vid(zz, xx, cc):
        return zz * (NX * NC) + xx * NC + cc

    zp, zm = (z + 1) % NZ, (z + NZ - 1) % NZ
    xp, xm = (x + 1) % NX, (x + NX - 1) % NX
    rp, rm, r2 = (r + 1) % NY, (r + NY - 1) % NY, (r + 2) % NY

    w_copy = pltpu.make_async_copy(w_hbm, W, loc.at[0])
    w_copy.start()
    own_copies = []
    for h in range(2):
        cp = pltpu.make_async_copy(hid.at[pl.ds(SHARD * h, SHARD)], G.at[h, z, x, c], loc.at[1 + h])
        cp.start()
        own_copies.append(cp)

    barrier = pltpu.get_barrier_semaphore()
    for ry in (rp, rm):
        pl.semaphore_signal(barrier, inc=1, device_id=(ry, v), device_id_type=MESH)

    @pl.loop(1, NV)
    def _(k):
        pl.semaphore_signal(barrier, inc=1, device_id=(r, (v + k) % NV), device_id_type=MESH)

    pl.semaphore_wait(barrier, NV + 1)

    sent = []

    def send(src, dst, ss, rs, dev):
        cp = pltpu.make_async_remote_copy(
            src_ref=src, dst_ref=dst, send_sem=ss, recv_sem=rs, device_id=dev, device_id_type=MESH
        )
        cp.start()
        sent.append(cp)

    def wait_recv(region, rs):
        pltpu.make_async_remote_copy(
            src_ref=region, dst_ref=region, send_sem=rs, recv_sem=rs, device_id=(r, v), device_id_type=MESH
        ).wait_recv()

    lo, hi = pl.ds(0, HALF_K), pl.ds(HALF_K, HALF_K)

    def x_start(h):
        own_copies[h].wait()
        mine = G.at[h, z, x, c]
        send(mine, mine, ag_send.at[h, 0], ag_recv.at[h, 0], (r, vid(z, xp, c)))
        send(mine, mine, ag_send.at[h, 1], ag_recv.at[h, 1], (r, vid(z, xm, c)))

    def x_mid(h):
        a = G.at[h, z, xm, c]
        wait_recv(a, ag_recv.at[h, 0])
        al = G.at[h, z, xm, c, :, lo]
        send(al, al, ag_send.at[h, 2], ag_recv.at[h, 2], (r, vid(z, xp, c)))
        b = G.at[h, z, xp, c]
        wait_recv(b, ag_recv.at[h, 1])
        bh = G.at[h, z, xp, c, :, hi]
        send(bh, bh, ag_send.at[h, 3], ag_recv.at[h, 3], (r, vid(z, xm, c)))

    def x_end(h):
        xo = (x + 2) % NX
        wait_recv(G.at[h, z, xo, c, :, lo], ag_recv.at[h, 2])
        wait_recv(G.at[h, z, xo, c, :, hi], ag_recv.at[h, 3])

    def sib(h, zz, slot):
        s = G.at[h, zz, :, c]
        send(s, s, ag_send.at[h, slot], ag_recv.at[h, slot], (r, vid(z, x, 1 - c)))

    def z_step(h, s):
        if s == 0:
            m = G.at[h, z, :, c]
            send(m, m, ag_send.at[h, 4], ag_recv.at[h, 4], (r, vid(zp, x, c)))
            send(m, m, ag_send.at[h, 5], ag_recv.at[h, 5], (r, vid(zm, x, c)))
            sib(h, z, 12)
            return
        za, zb = (z + NZ - s) % NZ, (z + s) % NZ
        if s < 4:
            a, b = G.at[h, za, :, c], G.at[h, zb, :, c]
            fa, fb = a, b
            if s == 3:
                fa, fb = G.at[h, za, :, c, :, lo], G.at[h, zb, :, c, :, hi]
            wait_recv(a, ag_recv.at[h, 2 + 2 * s])
            send(fa, fa, ag_send.at[h, 4 + 2 * s], ag_recv.at[h, 4 + 2 * s], (r, vid(zp, x, c)))
            wait_recv(b, ag_recv.at[h, 3 + 2 * s])
            send(fb, fb, ag_send.at[h, 5 + 2 * s], ag_recv.at[h, 5 + 2 * s], (r, vid(zm, x, c)))
            sib(h, za, 11 + 2 * s)
            sib(h, zb, 12 + 2 * s)
        else:
            wait_recv(G.at[h, za, :, c, :, lo], ag_recv.at[h, 10])
            wait_recv(G.at[h, za, :, c, :, hi], ag_recv.at[h, 11])
            sib(h, za, 19)

    def sib_wait(h):
        o = 1 - c
        wait_recv(G.at[h, z, :, o], ag_recv.at[h, 12])
        for s in range(1, 4):
            wait_recv(G.at[h, (z + NZ - s) % NZ, :, o], ag_recv.at[h, 11 + 2 * s])
            wait_recv(G.at[h, (z + s) % NZ, :, o], ag_recv.at[h, 12 + 2 * s])
        wait_recv(G.at[h, (z + 4) % NZ, :, o], ag_recv.at[h, 19])

    def product(h, which, owner):
        @pl.loop(0, 4)
        def _(n):
            lhs = G[h, pl.ds(2 * owner, 2)].reshape(256, 2 * HALF_K)
            rhs = W[:, pl.ds(pl.multiple_of(n * 256, 256), 256)]
            res = jnp.dot(lhs, rhs, preferred_element_type=F32)
            part[h, which, n // 2, :, pl.ds(pl.multiple_of((n % 2) * 256, 256), 256)] = res

    def far(h):
        product(h, 0, r2)
        send(part.at[h, 0, 0], leg.at[h, 0], y_send.at[h, 0], y_recv.at[h, 0], (rp, v))
        send(part.at[h, 0, 1], leg.at[h, 1], y_send.at[h, 1], y_recv.at[h, 1], (rm, v))

    def near(h):
        product(h, 1, rp)
        send(part.at[h, 1, 1], fin.at[h, 0, 1], y_send.at[h, 2], y_recv.at[h, 2], (rp, v))
        product(h, 2, rm)
        send(part.at[h, 2, 0], fin.at[h, 1, 0], y_send.at[h, 3], y_recv.at[h, 3], (rm, v))

    def onward(h):
        wait_recv(leg.at[h, 0], y_recv.at[h, 0])
        part[h, 1, 0] = part[h, 1, 0] + leg[h, 0]
        send(part.at[h, 1, 0], fin.at[h, 0, 0], y_send.at[h, 4], y_recv.at[h, 4], (rp, v))
        wait_recv(leg.at[h, 1], y_recv.at[h, 1])
        part[h, 2, 1] = part[h, 2, 1] + leg[h, 1]
        send(part.at[h, 2, 1], fin.at[h, 1, 1], y_send.at[h, 5], y_recv.at[h, 5], (rm, v))

    def fin_wait(h):
        wait_recv(fin.at[h, 0, 1], y_recv.at[h, 2])
        wait_recv(fin.at[h, 1, 0], y_recv.at[h, 3])
        wait_recv(fin.at[h, 0, 0], y_recv.at[h, 4])
        wait_recv(fin.at[h, 1, 1], y_recv.at[h, 5])

    def exchange_z(h, e):
        mine = S1.at[h, e, z]
        for k in range(1, NZ):
            pltpu.make_async_remote_copy(
                src_ref=mine, dst_ref=mine, send_sem=st_send.at[h, e, 0], recv_sem=st_recv.at[h, e, 0],
                device_id=(r, vid((z + k) % NZ, x, c)), device_id_type=MESH,
            ).start()

    def exchange_x(h, e):
        mine = S2.at[h, e, xc]
        for k in range(1, 8):
            pltpu.make_async_remote_copy(
                src_ref=mine, dst_ref=mine, send_sem=st_send.at[h, e, 1], recv_sem=st_recv.at[h, e, 1],
                device_id=(r, z * 8 + (xc + k) % 8), device_id_type=MESH,
            ).start()

    def exchange_wait(h, e, stage):
        buf = (S1, S2)[stage]
        wait_recv(buf.at[h, e, pl.ds(0, 7)], st_recv.at[h, e, stage])

    def exchange_sent(h, e, stage):
        buf = (S1, S2)[stage]
        region = buf.at[h, e, pl.ds(0, 7)]
        pltpu.make_async_remote_copy(
            src_ref=region, dst_ref=region, send_sem=st_send.at[h, e, stage], recv_sem=st_recv.at[h, e, stage],
            device_id=(r, v), device_id_type=MESH,
        ).wait_send()

    def local_stats(h):
        @pl.loop(0, 8)
        def _(i):
            rows = pl.ds(pl.multiple_of(i * 32, 32), 32)
            halves = []
            for q in range(2):
                halves.append(part[h, 3, q, rows] + (fin[h, 0, q, rows] + fin[h, 1, q, rows]))
            logit = jnp.concatenate(halves, axis=1)
            top = jnp.max(logit, axis=1, keepdims=True)
            weight = jnp.exp(logit - top)
            E[h, pl.ds(2 * i, 2)] = weight.reshape(2, SHARD, 1024)
            colm[h, rows] = jnp.broadcast_to(top, (32, 128))
            cola[rows] = fold8(weight)

        S1[h, 0, z, 0:1] = rows_to_lanes(colm.at[h])[0:1]
        S1[h, 0, z, 1:2] = jnp.sum(rows_to_lanes(cola), axis=0, keepdims=True)

    def merge_top(buf, h):
        tops = buf[h, 0, :, 0, :]
        sums = buf[h, 0, :, 1, :]
        top = jnp.max(tops, axis=0, keepdims=True)
        return top, jnp.sum(sums * jnp.exp(tops - top), axis=0, keepdims=True)

    def middle_top(h):
        exchange_wait(h, 0, 0)
        top, total = merge_top(S1, h)
        S2[h, 0, xc, 0:1] = top
        S2[h, 0, xc, 1:2] = total

    columns = (lax.broadcasted_iota(jnp.int32, (32, 1024), 1) + v * 1024).astype(F32)

    def local_excess(h):
        exchange_wait(h, 0, 1)
        top, total = merge_top(S2, h)
        own_top = rows_to_lanes(colm.at[h])[0:1]
        colm[h] = lanes_to_rows(jnp.exp(own_top - top) / total)

        @pl.loop(0, 8)
        def _(i):
            rows = pl.ds(pl.multiple_of(i * 32, 32), 32)
            two = pl.ds(2 * i, 2)
            target = E[h, two].reshape(32, 1024) * tile8(colm[h, rows])
            draft = dr[two, h].reshape(32, 1024)
            chosen = columns == tile8(idc[two, h].reshape(32, 128))
            excess = jnp.maximum(target - draft, 0.0)
            E[h, two] = excess.reshape(2, SHARD, 1024)
            cola[rows] = fold8(excess)
            colb[rows] = fold8(jnp.where(chosen, target, 0.0))
            colc[rows] = fold8(jnp.where(chosen, draft, 0.0))

        for k, ref in enumerate((cola, colb, colc)):
            S1[h, 1, z, k : k + 1] = jnp.sum(rows_to_lanes(ref), axis=0, keepdims=True)

    def middle_mass(h):
        exchange_wait(h, 1, 0)
        for k in range(3):
            S2[h, 1, xc, k : k + 1] = jnp.sum(S1[h, 1, :, k, :], axis=0, keepdims=True)

    def finish(h):
        exchange_wait(h, 1, 1)
        mass, picked, drafted = (jnp.sum(S2[h, 1, :, k, :], axis=0, keepdims=True) for k in range(3))
        acc_ref[h : h + 1] = jnp.minimum(1.0, picked / drafted)
        colm[h] = lanes_to_rows(1.0 / jnp.maximum(mass, mass_floor))

        @pl.loop(0, 8)
        def _(i):
            rows = pl.ds(pl.multiple_of(i * 32, 32), 32)
            two = pl.ds(2 * i, 2)
            scaled = E[h, two].reshape(32, 1024) * tile8(colm[h, rows])
            E[h, two] = scaled.reshape(2, SHARD, 1024)

        cp = pltpu.make_async_copy(E.at[h], out_hbm.at[:, h], loc.at[3 + h])
        cp.start()
        return cp

    spot = dr.at[v // 4, (v // 2) % 2, pl.ds(pl.multiple_of((v % 2) * 8, 8), 8)]

    def draft_send():
        pltpu.make_async_copy(draft_hbm.at[:, pl.ds(pl.multiple_of(v * 1024, 1024), 1024)], spot, dr_recv).start()

        @pl.loop(1, NV)
        def _(k):
            d = (v + k) % NV
            pltpu.make_async_remote_copy(
                src_ref=draft_hbm.at[:, pl.ds(pl.multiple_of(d * 1024, 1024), 1024)],
                dst_ref=spot, send_sem=dr_send, recv_sem=dr_recv, device_id=(r, d), device_id_type=MESH,
            ).start()

    x_start(0)
    x_start(1)
    x_mid(0)
    x_end(0)
    z_step(0, 0)
    x_mid(1)
    x_end(1)
    for j in range(4):
        row = ids_ref[j : j + 1].astype(F32)
        idc[4 * j : 4 * j + 4] = lanes_to_rows(row).reshape(4, 2, SHARD, 128)
    for s in range(1, 5):
        z_step(0, s)
    z_step(1, 0)
    w_copy.wait()
    sib_wait(0)
    far(0)
    z_step(1, 1)
    near(0)
    z_step(1, 2)
    product(0, 3, r)
    z_step(1, 3)
    z_step(1, 4)
    sib_wait(1)
    onward(0)
    far(1)
    near(1)
    draft_send()
    product(1, 3, r)
    fin_wait(0)
    local_stats(0)
    exchange_z(0, 0)
    middle_top(0)
    exchange_x(0, 0)
    onward(1)
    pltpu.make_async_copy(dr, dr, dr_recv).wait()
    local_excess(0)
    exchange_z(0, 1)
    middle_mass(0)
    exchange_x(0, 1)
    out0 = finish(0)
    fin_wait(1)
    local_stats(1)
    exchange_z(1, 0)
    middle_top(1)
    exchange_x(1, 0)
    local_excess(1)
    exchange_z(1, 1)
    middle_mass(1)
    exchange_x(1, 1)
    out1 = finish(1)

    for cp in sent:
        cp.wait_send()
    for h in range(2):
        for e in range(2):
            for stage in range(2):
                exchange_sent(h, e, stage)
    some = draft_hbm.at[:, pl.ds(0, (NV - 1) * 1024)]
    pltpu.make_async_remote_copy(
        src_ref=some, dst_ref=some, send_sem=dr_send, recv_sem=dr_recv, device_id=(r, v), device_id_type=MESH
    ).wait_send()
    out0.wait()
    out1.wait()


def local(hidden, head_weight, draft_probs, draft_ids):
    dma = pltpu.SemaphoreType.DMA
    residual, accept = pl.pallas_call(
        kernel,
        out_shape=(
            jax.ShapeDtypeStruct((16, 2, SHARD, 1024), F32),
            jax.ShapeDtypeStruct((2, 256), F32),
        ),
        in_specs=[pl.BlockSpec(memory_space=pl.ANY)] * 3 + [pl.BlockSpec(memory_space=pltpu.VMEM)],
        out_specs=(pl.BlockSpec(memory_space=pl.ANY), pl.BlockSpec(memory_space=pltpu.VMEM)),
        scratch_shapes=[
            pltpu.VMEM((2, NZ, NX, NC, SHARD, 2 * HALF_K), jnp.bfloat16),
            pltpu.VMEM((2 * HALF_K, 1024), jnp.bfloat16),
            pltpu.VMEM((2, 4, 2, 256, 512), F32),
            pltpu.VMEM((2, 2, 256, 512), F32),
            pltpu.VMEM((2, 2, 2, 256, 512), F32),
            pltpu.VMEM((16, 2, SHARD, 1024), F32),
            pltpu.VMEM((2, 16, SHARD, 1024), F32),
            pltpu.VMEM((16, 2, SHARD, 128), F32),
            pltpu.VMEM((2, 256, 128), F32),
            pltpu.VMEM((256, 128), F32),
            pltpu.VMEM((256, 128), F32),
            pltpu.VMEM((256, 128), F32),
            pltpu.VMEM((2, 2, 8, 8, 256), F32),
            pltpu.VMEM((2, 2, 8, 8, 256), F32),
            dma((2, 20)),
            dma((2, 20)),
            dma((2, 6)),
            dma((2, 6)),
            dma((2, 2, 2)),
            dma((2, 2, 2)),
            dma,
            dma,
            dma((5,)),
        ],
        compiler_params=pltpu.CompilerParams(
            collective_id=0, has_side_effects=True, vmem_limit_bytes=48 * 1024 * 1024
        ),
        cost_estimate=pl.CostEstimate(flops=7_516_192_768, bytes_accessed=16_000_000, transcendentals=524_288),
    )(hidden, head_weight, draft_probs, draft_ids.reshape(4, 128))
    accept = accept.reshape(2, 16, SHARD).transpose(1, 0, 2).reshape(512)
    return residual.reshape(512, 1024), accept


def solution(mesh):
    in_specs = (P("vocab", "rows"), P("rows", "vocab"), P(("rows", "vocab"), None), P("rows", None))
    out_specs = (P("rows", "vocab"), P("rows"))
    return jax.shard_map(local, mesh=mesh, in_specs=in_specs, out_specs=out_specs, check_vma=False)
```

```python
import jax
import jax.numpy as jnp
from jax import lax
from jax.experimental import pallas as pl
from jax.experimental.pallas import tpu as pltpu
from jax.sharding import PartitionSpec as P

MESH = pl.DeviceIdType.MESH
F32 = jnp.float32
mass_floor = 0.05

NY, NZ, NX, NC = 4, 8, 4, 2
NV = NZ * NX * NC
SHARD = 32
FEATURES = 1792
SPLIT = 1024
WIDTH = 1024
HALF = 512
ROWS = 256

ZF = pl.ds(0, SPLIT)
ZF_LO, ZF_HI = pl.ds(0, SPLIT // 2), pl.ds(SPLIT // 2, SPLIT // 2)
XF = pl.ds(SPLIT, FEATURES - SPLIT)
XF_LO = pl.ds(SPLIT, (FEATURES - SPLIT) // 2)
XF_HI = pl.ds((FEATURES + SPLIT) // 2, (FEATURES - SPLIT) // 2)

LEVELS = 8388600.0
STEPS = 64.0
PACKED = 384

ZZ, ZX, XX, XZ, SIB, AG_SEMS = 0, 8, 40, 44, 60, 68


def to_lanes(block):
    return jnp.transpose(block, (1, 0))


def to_rows(row):
    return jnp.transpose(jnp.broadcast_to(row, (128, row.shape[1])), (1, 0))


def tile8(block):
    return jnp.concatenate([block] * 8, axis=1)


def fold8(block):
    total = block[:, 0:128]
    for i in range(1, 8):
        total = total + block[:, 128 * i : 128 * (i + 1)]
    return total


def unpack(words, scale):
    a, b, c = (words[:, 128 * i : 128 * (i + 1)] for i in range(3))
    d = (a & 255) | ((b & 255) << 8) | ((c << 24) >> 8)
    return jnp.concatenate([q.astype(F32) * scale for q in (a >> 8, b >> 8, c >> 8, d)], axis=1)


def kernel(
    hid, w_hbm, draft_hbm, ids_ref, out_hbm, acc_ref,
    G, W, part, leg, fin, pk, dr, E, idc, colm, cola, colb, colc, colk, S,
    ag_send, ag_recv, y_send, y_recv, st_send, st_recv, dr_send, dr_recv, loc,
):
    r = lax.axis_index("rows")
    v = lax.axis_index("vocab")
    z = v // (NX * NC)
    x = (v // NC) % NX
    c = v % NC

    def vid(zz, xx, cc):
        return zz * (NX * NC) + xx * NC + cc

    def around(d):
        return (z + NZ + d) % NZ

    zp, zm = around(1), around(-1)
    xp, xm, xo = (x + 1) % NX, (x + NX - 1) % NX, (x + 2) % NX
    rp, rm = (r + 1) % NY, (r + NY - 1) % NY
    to_zp, to_zm = (r, vid(zp, x, c)), (r, vid(zm, x, c))
    to_xp, to_xm = (r, vid(z, xp, c)), (r, vid(z, xm, c))
    to_sib = (r, vid(z, x, 1 - c))
    order = [around(d) for d in (0, -1, 1, -2, 2, -3, 3, 4)]

    own_copy = pltpu.make_async_copy(hid, G.at[z, x, c], loc.at[0])
    own_copy.start()
    w_copy = pltpu.make_async_copy(w_hbm, W, loc.at[1])
    w_copy.start()

    barrier = pltpu.get_barrier_semaphore()
    for ry in (rp, rm):
        pl.semaphore_signal(barrier, inc=1, device_id=(ry, v), device_id_type=MESH)

    @pl.loop(1, NV)
    def _(k):
        pl.semaphore_signal(barrier, inc=1, device_id=(r, (v + k) % NV), device_id_type=MESH)

    pl.semaphore_wait(barrier, NV + 1)

    sent = []

    def remote(src, dst, ss, rs, dev):
        return pltpu.make_async_remote_copy(
            src_ref=src, dst_ref=dst, send_sem=ss, recv_sem=rs, device_id=dev, device_id_type=MESH
        )

    def wait_recv(region, rs):
        remote(region, region, rs, rs, to_sib).wait_recv()

    def spread(region, sem, dev, src=None):
        cp = remote(region if src is None else src, region, ag_send.at[sem], ag_recv.at[sem], dev)
        cp.start()
        sent.append(cp)

    def arrived(region, sem):
        wait_recv(region, ag_recv.at[sem])

    def zf(zz, xx, cols=ZF):
        return G.at[zz, xx, c, :, cols]

    def zf_x_send(j):
        src = hid.at[:, ZF] if j == 0 else None
        spread(zf(order[j], x), ZX + 4 * j, to_xp, src)
        spread(zf(order[j], x), ZX + 4 * j + 1, to_xm, src)

    def zf_x_mid(j):
        zz = order[j]
        arrived(zf(zz, xm), ZX + 4 * j)
        spread(zf(zz, xm, ZF_LO), ZX + 4 * j + 2, to_xp)
        arrived(zf(zz, xp), ZX + 4 * j + 1)
        spread(zf(zz, xp, ZF_HI), ZX + 4 * j + 3, to_xm)

    def zf_x_end(j):
        zz = order[j]
        arrived(zf(zz, xo, ZF_LO), ZX + 4 * j + 2)
        arrived(zf(zz, xo, ZF_HI), ZX + 4 * j + 3)

    def zf_z(d):
        if d == 0:
            spread(zf(z, x), ZZ, to_zp, hid.at[:, ZF])
            spread(zf(z, x), ZZ + 1, to_zm, hid.at[:, ZF])
            zf_x_send(0)
            return
        if d == 4:
            arrived(zf(order[7], x, ZF_LO), ZZ + 6)
            arrived(zf(order[7], x, ZF_HI), ZZ + 7)
            zf_x_send(7)
            return
        za, zb = order[2 * d - 1], order[2 * d]
        arrived(zf(za, x), ZZ + 2 * d - 2)
        spread(zf(za, x, ZF_LO if d == 3 else ZF), ZZ + 2 * d, to_zp)
        zf_x_send(2 * d - 1)
        arrived(zf(zb, x), ZZ + 2 * d - 1)
        spread(zf(zb, x, ZF_HI if d == 3 else ZF), ZZ + 2 * d + 1, to_zm)
        zf_x_send(2 * d)

    def xf(xx, cols=XF):
        return G.at[z, xx, c, :, cols]

    def xfs(zz, cols=XF):
        return G.at[zz, :, c, :, cols]

    def xf_x_start():
        spread(xf(x), XX, to_xp, hid.at[:, XF])
        spread(xf(x), XX + 1, to_xm, hid.at[:, XF])
        spread(xf(x), XX + 2, (r, vid(z, xo, c)), hid.at[:, XF])

    def xf_x_end():
        arrived(xf(xm), XX)
        arrived(xf(xp), XX + 1)
        arrived(xf(xo), XX + 2)

    def xf_z(d):
        if d == 0:
            spread(xfs(z, XF_LO), XZ, to_zp)
            spread(xfs(z, XF_HI), XZ + 3, to_zm)
            spread(xfs(z, XF_HI), XZ + 1, to_zp)
            spread(xfs(z, XF_LO), XZ + 2, to_zm)
            return
        if d == 4:
            arrived(xfs(order[7], XF_LO), XZ + 12)
            arrived(xfs(order[7], XF_HI), XZ + 13)
            return
        za, zb = order[2 * d - 1], order[2 * d]
        o = XZ + 4 * d
        arrived(xfs(za, XF_LO), o - 4)
        spread(xfs(za, XF_LO), o, to_zp)
        arrived(xfs(zb, XF_HI), o - 1)
        spread(xfs(zb, XF_HI), o + (1 if d == 3 else 3), to_zm)
        arrived(xfs(za, XF_HI), o - 3)
        arrived(xfs(zb, XF_LO), o - 2)
        if d < 3:
            spread(xfs(za, XF_HI), o + 1, to_zp)
            spread(xfs(zb, XF_LO), o + 2, to_zm)

    def sib(j):
        spread(G.at[order[j], :, c], SIB + j, to_sib)

    def sib_wait(j):
        arrived(G.at[order[j], :, 1 - c], SIB + j)

    def role(zz):
        return (zz // 2 - r + NY) % NY, zz % 2

    def far_left(q, j):
        return remote(pk.at[0, q, 0], leg.at[0, q], y_send.at[2 * j], y_recv.at[q], (rp, v))

    def far_right(q, j):
        return remote(pk.at[0, q, 1], leg.at[1, q], y_send.at[2 * j + 1], y_recv.at[2 + q], (rm, v))

    def near_right(q, j):
        return remote(pk.at[1, q, 1], fin.at[q, 0, 1], y_send.at[2 * j + 1], y_recv.at[4 + q], (rp, v))

    def near_left(q, j):
        return remote(pk.at[1, q, 0], fin.at[q, 1, 0], y_send.at[2 * j], y_recv.at[6 + q], (rm, v))

    def pack(zz, side, dst):
        @pl.loop(0, 4)
        def _(i):
            rows = pl.ds(pl.multiple_of(i * 64, 64), 64)
            block = part[zz, side, rows]
            unit = jnp.floor(jnp.max(jnp.abs(block), axis=1, keepdims=True) * STEPS) + 1.0
            colk[0, rows] = jnp.broadcast_to(unit, (64, 128))
            level = jnp.round(block * (LEVELS * STEPS / unit)).astype(jnp.int32)
            a, b, c, d = (level[:, 128 * k : 128 * (k + 1)] for k in range(4))
            dst[rows, 0:128] = (a << 8) | (d & 255)
            dst[rows, 128:256] = (b << 8) | ((d >> 8) & 255)
            dst[rows, 256:384] = (c << 8) | ((d >> 16) & 255)

        dst[ROWS : ROWS + 1, 0:ROWS] = to_lanes(colk[0])[0:1].astype(jnp.int32)

    def scales(src, k):
        colk[k] = to_rows(src[ROWS : ROWS + 1, 0:ROWS].astype(F32)) * (1.0 / (LEVELS * STEPS))

    def product(j):
        zz = order[j]

        @pl.loop(0, 4)
        def _(n):
            lhs = G[zz].reshape(ROWS, FEATURES)
            rhs = W[:, pl.ds(pl.multiple_of(n * 256, 256), 256)]
            res = jnp.dot(lhs, rhs, preferred_element_type=F32)
            part[zz, n // 2, :, pl.ds(pl.multiple_of((n % 2) * 256, 256), 256)] = res

        d, q = role(zz)

        @pl.when(d == 2)
        def _():
            pack(zz, 0, pk.at[0, q, 0])
            far_left(q, j).start()
            pack(zz, 1, pk.at[0, q, 1])
            far_right(q, j).start()

        @pl.when(d == 1)
        def _():
            pack(zz, 1, pk.at[1, q, 1])
            near_right(q, j).start()

        @pl.when(d == 3)
        def _():
            pack(zz, 0, pk.at[1, q, 0])
            near_left(q, j).start()

    def product_sent(j):
        d, q = role(order[j])

        @pl.when(d >= 2)
        def _():
            far_left(q, j).wait_send()

        @pl.when((d == 1) | (d == 2))
        def _():
            far_right(q, j).wait_send()

    def add_leg(zz, side, q):
        scales(leg.at[side, q], 1)

        @pl.loop(0, 4)
        def _(i):
            rows = pl.ds(pl.multiple_of(i * 64, 64), 64)
            part[zz, side, rows] = part[zz, side, rows] + unpack(leg[side, q, rows], colk[1, rows])

    def onward(q):
        for side, owner in ((0, rp), (1, rm)):
            zz = 2 * owner + q
            wait_recv(leg.at[side, q], y_recv.at[2 * side + q])
            add_leg(zz, side, q)
            pack(zz, side, pk.at[2, q, side])
            cp = remote(
                pk.at[2, q, side], fin.at[q, side, side], y_send.at[16 + 2 * side + q],
                y_recv.at[8 + 2 * side + q], (owner, v),
            )
            cp.start()
            sent.append(cp)

    def fin_wait(q):
        wait_recv(fin.at[q, 0, 1], y_recv.at[4 + q])
        wait_recv(fin.at[q, 1, 0], y_recv.at[6 + q])
        wait_recv(fin.at[q, 0, 0], y_recv.at[8 + q])
        wait_recv(fin.at[q, 1, 1], y_recv.at[10 + q])

    def exchange(q, e):
        mine = S.at[q, e, v]

        @pl.loop(0, NZ)
        def _(i):
            dz = 4 + (1 - 2 * (i % 2)) * ((i + 1) // 2)
            zz = (z + dz) % NZ
            for dx in (2, 1, 3, 0):
                for dc in (1, 0):
                    cp = remote(
                        mine, mine, st_send.at[q, e], st_recv.at[q, e],
                        (r, vid(zz, (x + dx) % NX, (c + dc) % NC)),
                    )
                    if dx == 0 and dc == 0:
                        pl.when(i < NZ - 1)(cp.start)
                    else:
                        cp.start()

    def exchange_wait(q, e):
        wait_recv(S.at[q, e, pl.ds(0, NV - 1)], st_recv.at[q, e])

    def exchange_sent(q, e):
        region = S.at[q, e, pl.ds(0, NV - 1)]
        remote(region, region, st_send.at[q, e], st_recv.at[q, e], to_sib).wait_send()

    def local_stats(q):
        zz = 2 * r + q
        for side in range(2):
            for k in range(2):
                scales(fin.at[q, k, side], 2 * side + k)

        @pl.loop(0, 8)
        def _(i):
            rows = pl.ds(pl.multiple_of(i * 32, 32), 32)
            halves = []
            for side in range(2):
                below = unpack(fin[q, 0, side, rows], colk[2 * side, rows])
                above = unpack(fin[q, 1, side, rows], colk[2 * side + 1, rows])
                halves.append(part[zz, side, rows] + (below + above))
            logit = jnp.concatenate(halves, axis=1)
            top = jnp.max(logit, axis=1, keepdims=True)
            weight = jnp.exp(logit - top)
            E[q, rows] = weight
            colm[q, rows] = jnp.broadcast_to(top, (32, 128))
            cola[rows] = fold8(weight)

        S[q, 0, v, :, 0:ROWS] = to_lanes(colm[q])[0:1]
        S[q, 0, v, :, ROWS : 2 * ROWS] = jnp.sum(to_lanes(cola[...]), axis=0, keepdims=True)

    columns = (lax.broadcasted_iota(jnp.int32, (32, WIDTH), 1) + v * WIDTH).astype(F32)

    def local_excess(q):
        exchange_wait(q, 0)
        tops = S[q, 0, :, :, 0:ROWS]
        sums = S[q, 0, :, :, ROWS : 2 * ROWS]
        top = jnp.max(tops, axis=0)
        total = jnp.sum(sums * jnp.exp(tops - top[None]), axis=0)
        own_top = to_lanes(colm[q])[0:1]
        colm[q] = to_rows(jnp.exp(own_top - top) / total)

        @pl.loop(0, 8)
        def _(i):
            rows = pl.ds(pl.multiple_of(i * 32, 32), 32)
            all_rows = pl.ds(pl.multiple_of(q * ROWS + i * 32, 32), 32)
            target = E[q, rows] * tile8(colm[q, rows])
            draft = dr[all_rows]
            chosen = columns == tile8(idc[all_rows])
            excess = jnp.maximum(target - draft, 0.0)
            E[q, rows] = excess
            cola[rows] = fold8(excess)
            colb[rows] = fold8(jnp.where(chosen, target, 0.0))
            colc[rows] = fold8(jnp.where(chosen, draft, 0.0))

        mass, picked, drafted = (
            jnp.sum(to_lanes(ref[...]), axis=0, keepdims=True) for ref in (cola, colb, colc)
        )
        token = jnp.concatenate([ids_ref[2 * q : 2 * q + 1], ids_ref[2 * q + 1 : 2 * q + 2]], axis=1)
        here = (token >= v * WIDTH) & (token < (v + 1) * WIDTH)
        ratio = jnp.where(here, jnp.minimum(1.0, picked / drafted), 0.0)
        S[q, 1, v, :, 0:ROWS] = mass
        S[q, 1, v, :, ROWS : 2 * ROWS] = ratio

    def finish(q):
        exchange_wait(q, 1)
        both = jnp.sum(S[q, 1], axis=0)
        acc_ref[q : q + 1] = both[:, ROWS : 2 * ROWS]
        colm[q] = to_rows(1.0 / jnp.maximum(both[:, 0:ROWS], mass_floor))

        @pl.loop(0, 8)
        def _(i):
            rows = pl.ds(pl.multiple_of(i * 32, 32), 32)
            E[q, rows] = E[q, rows] * tile8(colm[q, rows])

        cp = pltpu.make_async_copy(E.at[q], out_hbm.at[pl.ds(q * ROWS, ROWS)], loc.at[2 + q])
        cp.start()
        return cp

    spot = dr.at[pl.ds(pl.multiple_of(v * 8, 8), 8)]

    def draft_send():
        pltpu.make_async_copy(
            draft_hbm.at[:, pl.ds(pl.multiple_of(v * WIDTH, WIDTH), WIDTH)], spot, dr_recv
        ).start()

        @pl.loop(1, NV)
        def _(k):
            d = (v + k) % NV
            remote(
                draft_hbm.at[:, pl.ds(pl.multiple_of(d * WIDTH, WIDTH), WIDTH)], spot, dr_send, dr_recv, (r, d)
            ).start()

    zf_z(0)
    xf_x_start()
    zf_x_mid(0)
    own_copy.wait()
    xf_x_end()
    xf_z(0)
    zf_z(1)
    zf_x_end(0)
    sib(0)
    zf_x_mid(1)
    zf_x_mid(2)
    zf_z(2)
    w_copy.wait()
    sib_wait(0)
    product(0)
    for d in (1, 2, 3):
        a, b = 2 * d - 1, 2 * d
        xf_z(d)
        zf_x_end(a)
        zf_x_end(b)
        sib(a)
        sib(b)
        if d == 1:
            for j in range(4):
                idc[128 * j : 128 * j + 128] = to_rows(ids_ref[j : j + 1].astype(F32))
        if d < 3:
            zf_x_mid(a + 2)
            zf_x_mid(b + 2)
            zf_z(d + 2)
        else:
            zf_x_mid(7)
            draft_send()
        sib_wait(a)
        product(a)
        sib_wait(b)
        product(b)
    xf_z(4)
    zf_x_end(7)
    sib(7)
    sib_wait(7)
    product(7)
    onward(0)
    onward(1)
    fin_wait(0)
    local_stats(0)
    exchange(0, 0)
    pltpu.make_async_copy(dr, dr, dr_recv).wait()
    local_excess(0)
    exchange(0, 1)
    out0 = finish(0)
    fin_wait(1)
    local_stats(1)
    exchange(1, 0)
    local_excess(1)
    exchange(1, 1)
    out1 = finish(1)

    for cp in sent:
        cp.wait_send()
    for j in range(8):
        product_sent(j)
    for q in range(2):
        for e in range(2):
            exchange_sent(q, e)
    some = draft_hbm.at[:, pl.ds(0, (NV - 1) * WIDTH)]
    remote(some, some, dr_send, dr_recv, to_sib).wait_send()
    out0.wait()
    out1.wait()


def local(hidden, head_weight, draft_probs, draft_ids):
    dma = pltpu.SemaphoreType.DMA
    residual, accept = pl.pallas_call(
        kernel,
        out_shape=(
            jax.ShapeDtypeStruct((2 * ROWS, WIDTH), F32),
            jax.ShapeDtypeStruct((2, ROWS), F32),
        ),
        in_specs=[pl.BlockSpec(memory_space=pltpu.HBM)] * 3 + [pl.BlockSpec(memory_space=pltpu.VMEM)],
        out_specs=(pl.BlockSpec(memory_space=pltpu.HBM), pl.BlockSpec(memory_space=pltpu.VMEM)),
        scratch_shapes=[
            pltpu.VMEM((NZ, NX, NC, SHARD, FEATURES), jnp.bfloat16),
            pltpu.VMEM((FEATURES, WIDTH), jnp.bfloat16),
            pltpu.VMEM((NZ, 2, ROWS, HALF), F32),
            pltpu.VMEM((2, 2, ROWS + 8, PACKED), jnp.int32),
            pltpu.VMEM((2, 2, 2, ROWS + 8, PACKED), jnp.int32),
            pltpu.VMEM((3, 2, 2, ROWS + 8, PACKED), jnp.int32),
            pltpu.VMEM((2 * ROWS, WIDTH), F32),
            pltpu.VMEM((2, ROWS, WIDTH), F32),
            pltpu.VMEM((2 * ROWS, 128), F32),
            pltpu.VMEM((2, ROWS, 128), F32),
            pltpu.VMEM((ROWS, 128), F32),
            pltpu.VMEM((ROWS, 128), F32),
            pltpu.VMEM((ROWS, 128), F32),
            pltpu.VMEM((4, ROWS, 128), F32),
            pltpu.VMEM((2, 2, NV, 1, 2 * ROWS), F32),
            dma((AG_SEMS,)),
            dma((AG_SEMS,)),
            dma((20,)),
            dma((12,)),
            dma((2, 2)),
            dma((2, 2)),
            dma,
            dma,
            dma((4,)),
        ],
        compiler_params=pltpu.CompilerParams(
            collective_id=0, has_side_effects=True, vmem_limit_bytes=48 * 1024 * 1024
        ),
        cost_estimate=pl.CostEstimate(flops=7_516_192_768, bytes_accessed=16_000_000, transcendentals=524_288),
    )(hidden, head_weight, draft_probs, draft_ids.reshape(4, 128))
    return residual, accept.reshape(2 * ROWS)


def solution(mesh):
    in_specs = (P("vocab", "rows"), P("rows", "vocab"), P(("rows", "vocab"), None), P("rows", None))
    out_specs = (P("rows", "vocab"), P("rows"))
    return jax.shard_map(local, mesh=mesh, in_specs=in_specs, out_specs=out_specs, check_vma=False)
```

```python
import math

import jax
import jax.numpy as jnp
from jax import lax
from jax.experimental import pallas as pl
from jax.experimental.pallas import tpu as pltpu
from jax.sharding import PartitionSpec as P

MESH = pl.DeviceIdType.MESH
F32 = jnp.float32
mass_floor = 0.05

NY, NZ, NX, NC = 4, 8, 4, 2
NV = NZ * NX * NC
SHARD = 32
FEATURES = 1792
SPLIT = 1024
WIDTH = 1024
HALF = 512
ROWS = 256

ZF = pl.ds(0, SPLIT)
ZF_LO, ZF_HI = pl.ds(0, SPLIT // 2), pl.ds(SPLIT // 2, SPLIT // 2)
XF = pl.ds(SPLIT, FEATURES - SPLIT)
XF_LO = pl.ds(SPLIT, (FEATURES - SPLIT) // 2)
XF_HI = pl.ds((FEATURES + SPLIT) // 2, (FEATURES - SPLIT) // 2)

LEVELS = 8388600.0
STEPS = 64.0
PACKED = 384
LOG_STEPS = 2.0**17 / math.log(2.0)
LOG_ZERO = 2.0**24 - 1.0

ZZ, ZX, XX, XZ, SIB, AG_SEMS = 0, 8, 40, 44, 60, 68


def to_lanes(block):
    return jnp.transpose(block, (1, 0))


def to_rows(row):
    return jnp.transpose(jnp.broadcast_to(row, (128, row.shape[1])), (1, 0))


def tile8(block):
    return jnp.concatenate([block] * 8, axis=1)


def fold8(block):
    total = block[:, 0:128]
    for i in range(1, 8):
        total = total + block[:, 128 * i : 128 * (i + 1)]
    return total


def pack4(level):
    a, b, c, d = (level[:, 128 * k : 128 * (k + 1)] for k in range(4))
    words = ((a << 8) | (d & 255), (b << 8) | ((d >> 8) & 255), (c << 8) | ((d >> 16) & 255))
    return jnp.concatenate(words, axis=1)


def unpack(words, scale):
    a, b, c = (words[:, 128 * i : 128 * (i + 1)] for i in range(3))
    d = (a & 255) | ((b & 255) << 8) | ((c << 24) >> 8)
    return jnp.concatenate([q.astype(F32) * scale for q in (a >> 8, b >> 8, c >> 8, d)], axis=1)


def kernel(
    hid, w_hbm, draft_hbm, ids_ref, out_hbm, acc_ref,
    G, W, part, leg, fin, pk, dbuf, dpk, dr, dd, E, idc, colm, cola, colb, colc, colk, S,
    ag_send, ag_recv, y_send, y_recv, st_send, st_recv, dr_send, dr_recv, loc,
):
    r = lax.axis_index("rows")
    v = lax.axis_index("vocab")
    z = v // (NX * NC)
    x = (v // NC) % NX
    c = v % NC

    def vid(zz, xx, cc):
        return zz * (NX * NC) + xx * NC + cc

    def around(d):
        return (z + NZ + d) % NZ

    zp, zm = around(1), around(-1)
    xp, xm, xo = (x + 1) % NX, (x + NX - 1) % NX, (x + 2) % NX
    rp, rm = (r + 1) % NY, (r + NY - 1) % NY
    to_zp, to_zm = (r, vid(zp, x, c)), (r, vid(zm, x, c))
    to_zp2, to_zm2 = (r, vid(around(2), x, c)), (r, vid(around(-2), x, c))
    to_xp, to_xm, to_xo = (r, vid(z, xp, c)), (r, vid(z, xm, c)), (r, vid(z, xo, c))
    to_sib = (r, vid(z, x, 1 - c))
    order = [around(d) for d in (0, -1, 1, -2, 2, -3, 3, 4)]

    own_copy = pltpu.make_async_copy(hid, G.at[z, x, c], loc.at[0])
    own_copy.start()
    w_copy = pltpu.make_async_copy(w_hbm, W, loc.at[1])
    w_copy.start()
    draft_copy = pltpu.make_async_copy(draft_hbm, dbuf, loc.at[4])
    draft_copy.start()

    barrier = pltpu.get_barrier_semaphore()
    for ry in (rp, rm):
        pl.semaphore_signal(barrier, inc=1, device_id=(ry, v), device_id_type=MESH)

    @pl.loop(1, NV)
    def _(k):
        pl.semaphore_signal(barrier, inc=1, device_id=(r, (v + k) % NV), device_id_type=MESH)

    pl.semaphore_wait(barrier, NV + 1)

    sent = []

    def remote(src, dst, ss, rs, dev):
        return pltpu.make_async_remote_copy(
            src_ref=src, dst_ref=dst, send_sem=ss, recv_sem=rs, device_id=dev, device_id_type=MESH
        )

    def wait_recv(region, rs):
        remote(region, region, rs, rs, to_sib).wait_recv()

    def spread(region, sem, dev, src=None):
        cp = remote(region if src is None else src, region, ag_send.at[sem], ag_recv.at[sem], dev)
        cp.start()
        sent.append(cp)

    def arrived(region, sem):
        wait_recv(region, ag_recv.at[sem])

    def zf(zz, xx, cols=ZF):
        return G.at[zz, xx, c, :, cols]

    def zf_x_send(j):
        src = hid.at[:, ZF] if j == 0 else None
        for k, dev in enumerate((to_xp, to_xm, to_xo)):
            spread(zf(order[j], x), ZX + 4 * j + k, dev, src)

    def zf_x_end(j):
        for k, xx in enumerate((xm, xp, xo)):
            arrived(zf(order[j], xx), ZX + 4 * j + k)

    def zf_z(d):
        if d == 0:
            for k, dev in enumerate((to_zp, to_zm, to_zp2, to_zm2)):
                spread(zf(z, x), ZZ + k, dev, hid.at[:, ZF])
            zf_x_send(0)
            return
        if d == 4:
            arrived(zf(order[7], x, ZF_LO), ZZ + 6)
            arrived(zf(order[7], x, ZF_HI), ZZ + 7)
            zf_x_send(7)
            return
        za, zb = order[2 * d - 1], order[2 * d]
        arrived(zf(za, x), ZZ + 2 * d - 2)
        if d == 2:
            spread(zf(za, x), ZZ + 4, to_zp)
            spread(zf(za, x, ZF_LO), ZZ + 6, to_zp2)
        zf_x_send(2 * d - 1)
        arrived(zf(zb, x), ZZ + 2 * d - 1)
        if d == 2:
            spread(zf(zb, x), ZZ + 5, to_zm)
            spread(zf(zb, x, ZF_HI), ZZ + 7, to_zm2)
        zf_x_send(2 * d)

    def xf(xx, cols=XF):
        return G.at[z, xx, c, :, cols]

    def xfs(zz, cols=XF):
        return G.at[zz, :, c, :, cols]

    def xf_x_start():
        spread(xf(x), XX, to_xp, hid.at[:, XF])
        spread(xf(x), XX + 1, to_xm, hid.at[:, XF])
        spread(xf(x), XX + 2, to_xo, hid.at[:, XF])

    def xf_x_end():
        arrived(xf(xm), XX)
        arrived(xf(xp), XX + 1)
        arrived(xf(xo), XX + 2)

    def xf_z(d):
        if d == 0:
            spread(xfs(z, XF_LO), XZ, to_zp)
            spread(xfs(z, XF_HI), XZ + 3, to_zm)
            spread(xfs(z, XF_HI), XZ + 1, to_zp)
            spread(xfs(z, XF_LO), XZ + 2, to_zm)
            return
        if d == 4:
            arrived(xfs(order[7], XF_LO), XZ + 12)
            arrived(xfs(order[7], XF_HI), XZ + 13)
            return
        za, zb = order[2 * d - 1], order[2 * d]
        o = XZ + 4 * d
        arrived(xfs(za, XF_LO), o - 4)
        spread(xfs(za, XF_LO), o, to_zp)
        arrived(xfs(zb, XF_HI), o - 1)
        spread(xfs(zb, XF_HI), o + (1 if d == 3 else 3), to_zm)
        arrived(xfs(za, XF_HI), o - 3)
        arrived(xfs(zb, XF_LO), o - 2)
        if d < 3:
            spread(xfs(za, XF_HI), o + 1, to_zp)
            spread(xfs(zb, XF_LO), o + 2, to_zm)

    def sib(j):
        spread(G.at[order[j], :, c], SIB + j, to_sib)

    def sib_wait(j):
        arrived(G.at[order[j], :, 1 - c], SIB + j)

    def role(zz):
        return (zz // 2 - r + NY) % NY, zz % 2

    def far_left(q, j):
        return remote(pk.at[0, q, 0], leg.at[0, q], y_send.at[2 * j], y_recv.at[q], (rp, v))

    def far_right(q, j):
        return remote(pk.at[0, q, 1], leg.at[1, q], y_send.at[2 * j + 1], y_recv.at[2 + q], (rm, v))

    def near_right(q, j):
        return remote(pk.at[1, q, 1], fin.at[q, 0, 1], y_send.at[2 * j + 1], y_recv.at[4 + q], (rp, v))

    def near_left(q, j):
        return remote(pk.at[1, q, 0], fin.at[q, 1, 0], y_send.at[2 * j], y_recv.at[6 + q], (rm, v))

    def pack(zz, side, dst):
        @pl.loop(0, 4)
        def _(i):
            rows = pl.ds(pl.multiple_of(i * 64, 64), 64)
            block = part[zz, side, rows]
            unit = jnp.floor(jnp.max(jnp.abs(block), axis=1, keepdims=True) * STEPS) + 1.0
            colk[0, rows] = jnp.broadcast_to(unit, (64, 128))
            level = jnp.round(block * (LEVELS * STEPS / unit)).astype(jnp.int32)
            dst[rows] = pack4(level)

        dst[ROWS : ROWS + 1, 0:ROWS] = to_lanes(colk[0])[0:1].astype(jnp.int32)

    def scales(src, k):
        colk[k] = to_rows(src[ROWS : ROWS + 1, 0:ROWS].astype(F32)) * (1.0 / (LEVELS * STEPS))

    def product(j):
        zz = order[j]

        lhs = G[zz].reshape(ROWS, FEATURES)
        for n in range(2):
            part[zz, n] = jnp.dot(lhs, W[:, HALF * n : HALF * (n + 1)], preferred_element_type=F32)

        d, q = role(zz)

        @pl.when(d == 2)
        def _():
            pack(zz, 0, pk.at[0, q, 0])
            far_left(q, j).start()
            pack(zz, 1, pk.at[0, q, 1])
            far_right(q, j).start()

        @pl.when(d == 1)
        def _():
            pack(zz, 1, pk.at[1, q, 1])
            near_right(q, j).start()

        @pl.when(d == 3)
        def _():
            pack(zz, 0, pk.at[1, q, 0])
            near_left(q, j).start()

    def product_sent(j):
        d, q = role(order[j])

        @pl.when(d >= 2)
        def _():
            far_left(q, j).wait_send()

        @pl.when((d == 1) | (d == 2))
        def _():
            far_right(q, j).wait_send()

    def add_leg(zz, side, q):
        scales(leg.at[side, q], 1)

        @pl.loop(0, 4)
        def _(i):
            rows = pl.ds(pl.multiple_of(i * 64, 64), 64)
            part[zz, side, rows] = part[zz, side, rows] + unpack(leg[side, q, rows], colk[1, rows])

    def steps_to(zz):
        up, down = (zz - z + NZ) % NZ, (z - zz + NZ) % NZ
        return jnp.minimum(up, down)

    def onward(side, nth):
        owner = (rp, rm)[side]
        second = (steps_to(2 * owner + 1) < steps_to(2 * owner)).astype(jnp.int32)
        q = second if nth == 0 else 1 - second
        zz = 2 * owner + q
        wait_recv(leg.at[side, q], y_recv.at[2 * side + q])
        add_leg(zz, side, q)
        pack(zz, side, pk.at[2, q, side])
        cp = remote(
            pk.at[2, q, side], fin.at[q, side, side], y_send.at[16 + 2 * side + q],
            y_recv.at[8 + 2 * side + q], (owner, v),
        )
        cp.start()
        sent.append(cp)

    def fin_wait(q):
        wait_recv(fin.at[q, 0, 1], y_recv.at[4 + q])
        wait_recv(fin.at[q, 1, 0], y_recv.at[6 + q])
        wait_recv(fin.at[q, 0, 0], y_recv.at[8 + q])
        wait_recv(fin.at[q, 1, 1], y_recv.at[10 + q])

    def exchange(q, e):
        mine = S.at[q, e, v]

        @pl.loop(0, NZ)
        def _(i):
            dz = 4 + (1 - 2 * (i % 2)) * ((i + 1) // 2)
            zz = (z + dz) % NZ
            for dx in (2, 1, 3, 0):
                for dc in (1, 0):
                    cp = remote(
                        mine, mine, st_send.at[q, e], st_recv.at[q, e],
                        (r, vid(zz, (x + dx) % NX, (c + dc) % NC)),
                    )
                    if dx == 0 and dc == 0:
                        pl.when(i < NZ - 1)(cp.start)
                    else:
                        cp.start()

    def exchange_wait(q, e):
        wait_recv(S.at[q, e, pl.ds(0, NV - 1)], st_recv.at[q, e])

    def exchange_sent(q, e):
        region = S.at[q, e, pl.ds(0, NV - 1)]
        remote(region, region, st_send.at[q, e], st_recv.at[q, e], to_sib).wait_send()

    def local_stats(q):
        zz = 2 * r + q
        for side in range(2):
            for k in range(2):
                scales(fin.at[q, k, side], 2 * side + k)

        @pl.loop(0, 8)
        def _(i):
            rows = pl.ds(pl.multiple_of(i * 32, 32), 32)
            halves = []
            for side in range(2):
                below = unpack(fin[q, 0, side, rows], colk[2 * side, rows])
                above = unpack(fin[q, 1, side, rows], colk[2 * side + 1, rows])
                halves.append(part[zz, side, rows] + (below + above))
            logit = jnp.concatenate(halves, axis=1)
            top = jnp.max(logit, axis=1, keepdims=True)
            weight = jnp.exp(logit - top)
            E[q, rows] = weight
            colm[q, rows] = jnp.broadcast_to(top, (32, 128))
            cola[rows] = fold8(weight)

        S[q, 0, v, :, 0:ROWS] = to_lanes(colm[q])[0:1]
        S[q, 0, v, :, ROWS : 2 * ROWS] = jnp.sum(to_lanes(cola[...]), axis=0, keepdims=True)

    columns = (lax.broadcasted_iota(jnp.int32, (32, WIDTH), 1) + v * WIDTH).astype(F32)

    def local_excess(q):
        exchange_wait(q, 0)
        tops = S[q, 0, :, :, 0:ROWS]
        sums = S[q, 0, :, :, ROWS : 2 * ROWS]
        top = jnp.max(tops, axis=0)
        total = jnp.sum(sums * jnp.exp(tops - top[None]), axis=0)
        own_top = to_lanes(colm[q])[0:1]
        colm[q] = to_rows(jnp.exp(own_top - top) / total)

        @pl.loop(0, 8)
        def _(i):
            rows = pl.ds(pl.multiple_of(i * 32, 32), 32)
            all_rows = pl.ds(pl.multiple_of(q * ROWS + i * 32, 32), 32)
            target = E[q, rows] * tile8(colm[q, rows])
            draft = dd[all_rows]
            chosen = columns == tile8(idc[all_rows])
            excess = jnp.maximum(target - draft, 0.0)
            E[q, rows] = excess
            cola[rows] = fold8(excess)
            colb[rows] = fold8(jnp.where(chosen, target, 0.0))
            colc[rows] = fold8(jnp.where(chosen, draft, 0.0))

        mass, picked, drafted = (
            jnp.sum(to_lanes(ref[...]), axis=0, keepdims=True) for ref in (cola, colb, colc)
        )
        token = jnp.concatenate([ids_ref[2 * q : 2 * q + 1], ids_ref[2 * q + 1 : 2 * q + 2]], axis=1)
        here = (token >= v * WIDTH) & (token < (v + 1) * WIDTH)
        ratio = jnp.where(here, jnp.minimum(1.0, picked / drafted), 0.0)
        S[q, 1, v, :, 0:ROWS] = mass
        S[q, 1, v, :, ROWS : 2 * ROWS] = ratio

    def finish(q):
        exchange_wait(q, 1)
        both = jnp.sum(S[q, 1], axis=0)
        acc_ref[q : q + 1] = both[:, ROWS : 2 * ROWS]
        colm[q] = to_rows(1.0 / jnp.maximum(both[:, 0:ROWS], mass_floor))

        @pl.loop(0, 8)
        def _(i):
            rows = pl.ds(pl.multiple_of(i * 32, 32), 32)
            E[q, rows] = E[q, rows] * tile8(colm[q, rows])

        cp = pltpu.make_async_copy(E.at[q], out_hbm.at[pl.ds(q * ROWS, ROWS)], loc.at[2 + q])
        cp.start()
        return cp

    spot = dr.at[pl.ds(pl.multiple_of(v * 8, 8), 8)]

    def draft_block(d):
        return dpk.at[:, pl.ds(pl.multiple_of(d * 768, 128), 768)]

    def draft_encode():
        draft_copy.wait()

        @pl.loop(0, 16)
        def _(i):
            block = dbuf[:, pl.ds(pl.multiple_of(i * 4096, 4096), 4096)]
            code = jnp.round(jnp.log(block) * -LOG_STEPS)
            code = jnp.minimum(jnp.maximum(code, 0.0), LOG_ZERO).astype(jnp.int32)
            words = [pack4(code[:, HALF * k : HALF * (k + 1)]) for k in range(8)]
            dpk[:, pl.ds(pl.multiple_of(i * 3072, 1024), 3072)] = jnp.concatenate(words, axis=1)

    def draft_send():
        pltpu.make_async_copy(draft_block(v), spot, dr_recv).start()

        @pl.loop(1, NV)
        def _(k):
            d = (v + k) % NV
            remote(draft_block(d), spot, dr_send, dr_recv, (r, d)).start()

    def draft_decode():
        pltpu.make_async_copy(dr, dr, dr_recv).wait()

        @pl.loop(0, 16)
        def _(i):
            rows = pl.ds(pl.multiple_of(i * 32, 32), 32)
            words = dr[rows]
            for k in range(2):
                w = words[:, PACKED * k : PACKED * (k + 1)]
                a, b, c = (w[:, 128 * j : 128 * (j + 1)] for j in range(3))
                d = (a & 255) | ((b & 255) << 8) | ((c & 255) << 16)
                for j, code in enumerate(((a >> 8) & 0xFFFFFF, (b >> 8) & 0xFFFFFF, (c >> 8) & 0xFFFFFF, d)):
                    code = code.astype(F32)
                    value = jnp.where(code < LOG_ZERO, jnp.exp(code * (-1.0 / LOG_STEPS)), 0.0)
                    dd[rows, HALF * k + 128 * j : HALF * k + 128 * (j + 1)] = value

    xf_x_start()
    zf_z(0)
    draft_encode()
    own_copy.wait()
    xf_x_end()
    xf_z(0)
    zf_z(1)
    zf_z(2)
    zf_x_end(0)
    sib(0)
    for j in range(4):
        idc[128 * j : 128 * j + 128] = to_rows(ids_ref[j : j + 1].astype(F32))
    zf_z(3)
    zf_z(4)
    w_copy.wait()
    sib_wait(0)
    product(0)
    for d in (1, 2, 3):
        a, b = 2 * d - 1, 2 * d
        xf_z(d)
        zf_x_end(a)
        sib(a)
        zf_x_end(b)
        sib(b)
        if d == 3:
            draft_send()
        sib_wait(a)
        product(a)
        sib_wait(b)
        product(b)
    xf_z(4)
    zf_x_end(7)
    sib(7)
    sib_wait(7)
    product(7)
    for nth in range(2):
        for side in range(2):
            onward(side, nth)
    draft_decode()
    fin_wait(0)
    local_stats(0)
    exchange(0, 0)
    fin_wait(1)
    local_stats(1)
    exchange(1, 0)
    local_excess(0)
    exchange(0, 1)
    local_excess(1)
    exchange(1, 1)
    out0 = finish(0)
    out1 = finish(1)

    for cp in sent:
        cp.wait_send()
    for j in range(8):
        product_sent(j)
    for q in range(2):
        for e in range(2):
            exchange_sent(q, e)
    some = dpk.at[:, pl.ds(0, (NV - 1) * 768)]
    remote(some, some, dr_send, dr_recv, to_sib).wait_send()
    out0.wait()
    out1.wait()


def local(hidden, head_weight, draft_probs, draft_ids):
    dma = pltpu.SemaphoreType.DMA
    residual, accept = pl.pallas_call(
        kernel,
        out_shape=(
            jax.ShapeDtypeStruct((2 * ROWS, WIDTH), F32),
            jax.ShapeDtypeStruct((2, ROWS), F32),
        ),
        in_specs=[pl.BlockSpec(memory_space=pltpu.HBM)] * 3 + [pl.BlockSpec(memory_space=pltpu.VMEM)],
        out_specs=(pl.BlockSpec(memory_space=pltpu.HBM), pl.BlockSpec(memory_space=pltpu.VMEM)),
        scratch_shapes=[
            pltpu.VMEM((NZ, NX, NC, SHARD, FEATURES), jnp.bfloat16),
            pltpu.VMEM((FEATURES, WIDTH), jnp.bfloat16),
            pltpu.VMEM((NZ, 2, ROWS, HALF), F32),
            pltpu.VMEM((2, 2, ROWS + 8, PACKED), jnp.int32),
            pltpu.VMEM((2, 2, 2, ROWS + 8, PACKED), jnp.int32),
            pltpu.VMEM((3, 2, 2, ROWS + 8, PACKED), jnp.int32),
            pltpu.VMEM((8, NV * WIDTH), F32),
            pltpu.VMEM((8, NV * 768), jnp.int32),
            pltpu.VMEM((2 * ROWS, 768), jnp.int32),
            pltpu.VMEM((2 * ROWS, WIDTH), F32),
            pltpu.VMEM((2, ROWS, WIDTH), F32),
            pltpu.VMEM((2 * ROWS, 128), F32),
            pltpu.VMEM((2, ROWS, 128), F32),
            pltpu.VMEM((ROWS, 128), F32),
            pltpu.VMEM((ROWS, 128), F32),
            pltpu.VMEM((ROWS, 128), F32),
            pltpu.VMEM((4, ROWS, 128), F32),
            pltpu.VMEM((2, 2, NV, 1, 2 * ROWS), F32),
            dma((AG_SEMS,)),
            dma((AG_SEMS,)),
            dma((20,)),
            dma((12,)),
            dma((2, 2)),
            dma((2, 2)),
            dma,
            dma,
            dma((5,)),
        ],
        compiler_params=pltpu.CompilerParams(
            collective_id=0, has_side_effects=True, vmem_limit_bytes=48 * 1024 * 1024
        ),
        cost_estimate=pl.CostEstimate(flops=7_516_192_768, bytes_accessed=16_000_000, transcendentals=524_288),
    )(hidden, head_weight, draft_probs, draft_ids.reshape(4, 128))
    return residual, accept.reshape(2 * ROWS)


def solution(mesh):
    in_specs = (P("vocab", "rows"), P("rows", "vocab"), P(("rows", "vocab"), None), P("rows", None))
    out_specs = (P("rows", "vocab"), P("rows"))
    return jax.shard_map(local, mesh=mesh, in_specs=in_specs, out_specs=out_specs, check_vma=False)
```

```python
import math

import jax
import jax.numpy as jnp
from jax import lax
from jax.experimental import pallas as pl
from jax.experimental.pallas import tpu as pltpu
from jax.sharding import PartitionSpec as P

MESH = pl.DeviceIdType.MESH
F32 = jnp.float32
mass_floor = 0.05

NY, NZ, NX, NC = 4, 8, 4, 2
NV = NZ * NX * NC
SHARD = 32
FEATURES = 1792
SPLIT = 1024
WIDTH = 1024
HALF = 512
ROWS = 256

ZF = pl.ds(0, SPLIT)
ZF_LO, ZF_HI = pl.ds(0, SPLIT // 2), pl.ds(SPLIT // 2, SPLIT // 2)
XF = pl.ds(SPLIT, FEATURES - SPLIT)
XF_LO = pl.ds(SPLIT, (FEATURES - SPLIT) // 2)
XF_HI = pl.ds((FEATURES + SPLIT) // 2, (FEATURES - SPLIT) // 2)

LEVELS = 8388600.0
STEPS = 64.0
PACKED = 384
LOG_STEPS = 2.0**17 / math.log(2.0)
LOG_ZERO = 2.0**24 - 1.0

ZZ, ZX, XX, XZ, SIB, AG_SEMS = 0, 8, 40, 44, 60, 68


def to_lanes(block):
    return jnp.transpose(block, (1, 0))


def to_rows(row):
    return jnp.transpose(jnp.broadcast_to(row, (128, row.shape[1])), (1, 0))


def tile8(block):
    return jnp.concatenate([block] * 8, axis=1)


def fold8(block):
    total = block[:, 0:128]
    for i in range(1, 8):
        total = total + block[:, 128 * i : 128 * (i + 1)]
    return total


def pack4(level):
    a, b, c, d = (level[:, 128 * k : 128 * (k + 1)] for k in range(4))
    words = ((a << 8) | (d & 255), (b << 8) | ((d >> 8) & 255), (c << 8) | ((d >> 16) & 255))
    return jnp.concatenate(words, axis=1)


def unpack(words, scale):
    a, b, c = (words[:, 128 * i : 128 * (i + 1)] for i in range(3))
    d = (a & 255) | ((b & 255) << 8) | ((c << 24) >> 8)
    return jnp.concatenate([q.astype(F32) * scale for q in (a >> 8, b >> 8, c >> 8, d)], axis=1)


def kernel(
    hid, w_hbm, draft_hbm, ids_ref, out_hbm, acc_ref,
    G, W, part, leg, fin, pk, dbuf, dpk, dr, dd, E, idc, colm, cola, colb, colc, colk, S,
    ag_send, ag_recv, y_send, y_recv, st_send, st_recv, dr_send, dr_recv, loc,
):
    r = lax.axis_index("rows")
    v = lax.axis_index("vocab")
    z = v // (NX * NC)
    x = (v // NC) % NX
    c = v % NC

    def vid(zz, xx, cc):
        return zz * (NX * NC) + xx * NC + cc

    def around(d):
        return (z + NZ + d) % NZ

    zp, zm = around(1), around(-1)
    xp, xm, xo = (x + 1) % NX, (x + NX - 1) % NX, (x + 2) % NX
    rp, rm = (r + 1) % NY, (r + NY - 1) % NY
    to_zp, to_zm = (r, vid(zp, x, c)), (r, vid(zm, x, c))
    to_zp2, to_zm2 = (r, vid(around(2), x, c)), (r, vid(around(-2), x, c))
    to_xp, to_xm, to_xo = (r, vid(z, xp, c)), (r, vid(z, xm, c)), (r, vid(z, xo, c))
    to_sib = (r, vid(z, x, 1 - c))
    order = [around(d) for d in (0, -1, 1, -2, 2, -3, 3, 4)]

    own_copy = pltpu.make_async_copy(hid, G.at[z, x, c], loc.at[0])
    own_copy.start()
    w_copy = pltpu.make_async_copy(w_hbm, W, loc.at[1])
    w_copy.start()
    draft_copy = pltpu.make_async_copy(draft_hbm, dbuf, loc.at[4])
    draft_copy.start()

    barrier = pltpu.get_barrier_semaphore()
    near = (to_zp, to_zm, to_zp2, to_zm2, to_xp, to_xm, to_xo, to_sib, (rp, v), (rm, v))
    for dev in near:
        pl.semaphore_signal(barrier, inc=1, device_id=dev, device_id_type=MESH)
    pl.semaphore_wait(barrier, len(near))

    sent = []

    def remote(src, dst, ss, rs, dev):
        return pltpu.make_async_remote_copy(
            src_ref=src, dst_ref=dst, send_sem=ss, recv_sem=rs, device_id=dev, device_id_type=MESH
        )

    def wait_recv(region, rs):
        remote(region, region, rs, rs, to_sib).wait_recv()

    def spread(region, sem, dev, src=None):
        cp = remote(region if src is None else src, region, ag_send.at[sem], ag_recv.at[sem], dev)
        cp.start()
        sent.append(cp)

    def arrived(region, sem):
        wait_recv(region, ag_recv.at[sem])

    def zf(zz, xx, cols=ZF):
        return G.at[zz, xx, c, :, cols]

    def zf_x_send(j):
        src = hid.at[:, ZF] if j == 0 else None
        for k, dev in enumerate((to_xp, to_xm, to_xo)):
            spread(zf(order[j], x), ZX + 4 * j + k, dev, src)

    def zf_x_end(j):
        for k, xx in enumerate((xm, xp, xo)):
            arrived(zf(order[j], xx), ZX + 4 * j + k)

    def zf_z(d):
        if d == 0:
            for k, dev in enumerate((to_zp, to_zm, to_zp2, to_zm2)):
                spread(zf(z, x), ZZ + k, dev, hid.at[:, ZF])
            zf_x_send(0)
            return
        if d == 4:
            arrived(zf(order[7], x, ZF_LO), ZZ + 6)
            arrived(zf(order[7], x, ZF_HI), ZZ + 7)
            zf_x_send(7)
            return
        za, zb = order[2 * d - 1], order[2 * d]
        arrived(zf(za, x), ZZ + 2 * d - 2)
        if d == 2:
            spread(zf(za, x), ZZ + 4, to_zp)
            spread(zf(za, x, ZF_LO), ZZ + 6, to_zp2)
        zf_x_send(2 * d - 1)
        arrived(zf(zb, x), ZZ + 2 * d - 1)
        if d == 2:
            spread(zf(zb, x), ZZ + 5, to_zm)
            spread(zf(zb, x, ZF_HI), ZZ + 7, to_zm2)
        zf_x_send(2 * d)

    def xf(xx, cols=XF):
        return G.at[z, xx, c, :, cols]

    def xfs(zz, cols=XF):
        return G.at[zz, :, c, :, cols]

    def xf_x_start():
        spread(xf(x), XX, to_xp, hid.at[:, XF])
        spread(xf(x), XX + 1, to_xm, hid.at[:, XF])
        spread(xf(x), XX + 2, to_xo, hid.at[:, XF])

    def xf_x_end():
        arrived(xf(xm), XX)
        arrived(xf(xp), XX + 1)
        arrived(xf(xo), XX + 2)

    def xf_z(d):
        if d == 0:
            spread(xfs(z, XF_LO), XZ, to_zp)
            spread(xfs(z, XF_HI), XZ + 3, to_zm)
            spread(xfs(z, XF_HI), XZ + 1, to_zp)
            spread(xfs(z, XF_LO), XZ + 2, to_zm)
            return
        if d == 4:
            arrived(xfs(order[7], XF_LO), XZ + 12)
            arrived(xfs(order[7], XF_HI), XZ + 13)
            return
        za, zb = order[2 * d - 1], order[2 * d]
        o = XZ + 4 * d
        arrived(xfs(za, XF_LO), o - 4)
        spread(xfs(za, XF_LO), o, to_zp)
        arrived(xfs(zb, XF_HI), o - 1)
        spread(xfs(zb, XF_HI), o + (1 if d == 3 else 3), to_zm)
        arrived(xfs(za, XF_HI), o - 3)
        arrived(xfs(zb, XF_LO), o - 2)
        if d < 3:
            spread(xfs(za, XF_HI), o + 1, to_zp)
            spread(xfs(zb, XF_LO), o + 2, to_zm)

    def sib(j):
        spread(G.at[order[j], :, c], SIB + j, to_sib)

    def sib_wait(j):
        arrived(G.at[order[j], :, 1 - c], SIB + j)

    def role(zz):
        return (zz // 2 - r + NY) % NY, zz % 2

    odd = z % 2
    far_down = (role(around(-2))[0] == 2).astype(jnp.int32)
    far_up = (role(around(2))[0] == 2).astype(jnp.int32)
    work = [z]
    for d in (1, 2, 3):
        up = odd if d != 2 else odd * far_up + (1 - odd) * (1 - far_down)
        work += [around(d * (2 * up - 1)), around(-d * (2 * up - 1))]
    work.append(order[7])

    def far_left(q, j):
        return remote(pk.at[0, q, 0], leg.at[0, q], y_send.at[2 * j], y_recv.at[q], (rp, v))

    def far_right(q, j):
        return remote(pk.at[0, q, 1], leg.at[1, q], y_send.at[2 * j + 1], y_recv.at[2 + q], (rm, v))

    def near_right(q, j):
        return remote(pk.at[1, q, 1], fin.at[q, 0, 1], y_send.at[2 * j + 1], y_recv.at[4 + q], (rp, v))

    def near_left(q, j):
        return remote(pk.at[1, q, 0], fin.at[q, 1, 0], y_send.at[2 * j], y_recv.at[6 + q], (rm, v))

    def pack(zz, side, dst):
        @pl.loop(0, 4)
        def _(i):
            rows = pl.ds(pl.multiple_of(i * 64, 64), 64)
            block = part[zz, side, rows]
            unit = jnp.floor(jnp.max(jnp.abs(block), axis=1, keepdims=True) * STEPS) + 1.0
            colk[0, rows] = jnp.broadcast_to(unit, (64, 128))
            level = jnp.round(block * (LEVELS * STEPS / unit)).astype(jnp.int32)
            dst[rows] = pack4(level)

        dst[ROWS : ROWS + 1, 0:ROWS] = to_lanes(colk[0])[0:1].astype(jnp.int32)

    def scales(src, k):
        colk[k] = to_rows(src[ROWS : ROWS + 1, 0:ROWS].astype(F32)) * (1.0 / (LEVELS * STEPS))

    def product(j):
        zz = work[j]

        lhs = G[zz].reshape(ROWS, FEATURES)
        for n in range(2):
            part[zz, n] = jnp.dot(lhs, W[:, HALF * n : HALF * (n + 1)], preferred_element_type=F32)

        d, q = role(zz)

        @pl.when(d == 2)
        def _():
            pack(zz, 0, pk.at[0, q, 0])
            far_left(q, j).start()
            pack(zz, 1, pk.at[0, q, 1])
            far_right(q, j).start()

        @pl.when(d == 1)
        def _():
            pack(zz, 1, pk.at[1, q, 1])
            near_right(q, j).start()

        @pl.when(d == 3)
        def _():
            pack(zz, 0, pk.at[1, q, 0])
            near_left(q, j).start()

    def product_sent(j):
        d, q = role(work[j])

        @pl.when(d >= 2)
        def _():
            far_left(q, j).wait_send()

        @pl.when((d == 1) | (d == 2))
        def _():
            far_right(q, j).wait_send()

    def add_leg(zz, side, q):
        scales(leg.at[side, q], 1)

        @pl.loop(0, 4)
        def _(i):
            rows = pl.ds(pl.multiple_of(i * 64, 64), 64)
            part[zz, side, rows] = part[zz, side, rows] + unpack(leg[side, q, rows], colk[1, rows])

    def steps_to(zz):
        up, down = (zz - z + NZ) % NZ, (z - zz + NZ) % NZ
        return jnp.minimum(up, down)

    def onward(side, nth):
        owner = (rp, rm)[side]
        second = (steps_to(2 * owner + 1) < steps_to(2 * owner)).astype(jnp.int32)
        q = second if nth == 0 else 1 - second
        zz = 2 * owner + q
        wait_recv(leg.at[side, q], y_recv.at[2 * side + q])
        add_leg(zz, side, q)
        pack(zz, side, pk.at[2, q, side])
        cp = remote(
            pk.at[2, q, side], fin.at[q, side, side], y_send.at[16 + 2 * side + q],
            y_recv.at[8 + 2 * side + q], (owner, v),
        )
        cp.start()
        sent.append(cp)

    def fin_wait(q):
        wait_recv(fin.at[q, 0, 1], y_recv.at[4 + q])
        wait_recv(fin.at[q, 1, 0], y_recv.at[6 + q])
        wait_recv(fin.at[q, 0, 0], y_recv.at[8 + q])
        wait_recv(fin.at[q, 1, 1], y_recv.at[10 + q])

    def exchange(q, e):
        mine = S.at[q, e, v]

        @pl.loop(0, NZ)
        def _(i):
            dz = 4 + (1 - 2 * (i % 2)) * ((i + 1) // 2)
            zz = (z + dz) % NZ
            for dx in (2, 1, 3, 0):
                for dc in (1, 0):
                    cp = remote(
                        mine, mine, st_send.at[q, e], st_recv.at[q, e],
                        (r, vid(zz, (x + dx) % NX, (c + dc) % NC)),
                    )
                    if dx == 0 and dc == 0:
                        pl.when(i < NZ - 1)(cp.start)
                    else:
                        cp.start()

    def exchange_wait(q, e):
        wait_recv(S.at[q, e, pl.ds(0, NV - 1)], st_recv.at[q, e])

    def exchange_sent(q, e):
        region = S.at[q, e, pl.ds(0, NV - 1)]
        remote(region, region, st_send.at[q, e], st_recv.at[q, e], to_sib).wait_send()

    def local_stats(q):
        zz = 2 * r + q
        for side in range(2):
            for k in range(2):
                scales(fin.at[q, k, side], 2 * side + k)

        @pl.loop(0, 8)
        def _(i):
            rows = pl.ds(pl.multiple_of(i * 32, 32), 32)
            halves = []
            for side in range(2):
                below = unpack(fin[q, 0, side, rows], colk[2 * side, rows])
                above = unpack(fin[q, 1, side, rows], colk[2 * side + 1, rows])
                halves.append(part[zz, side, rows] + (below + above))
            logit = jnp.concatenate(halves, axis=1)
            top = jnp.max(logit, axis=1, keepdims=True)
            weight = jnp.exp(logit - top)
            E[q, rows] = weight
            colm[q, rows] = jnp.broadcast_to(top, (32, 128))
            cola[rows] = fold8(weight)

        S[q, 0, v, :, 0:ROWS] = to_lanes(colm[q])[0:1]
        S[q, 0, v, :, ROWS : 2 * ROWS] = jnp.sum(to_lanes(cola[...]), axis=0, keepdims=True)

    columns = (lax.broadcasted_iota(jnp.int32, (32, WIDTH), 1) + v * WIDTH).astype(F32)

    def local_excess(q):
        exchange_wait(q, 0)
        tops = S[q, 0, :, :, 0:ROWS]
        sums = S[q, 0, :, :, ROWS : 2 * ROWS]
        top = jnp.max(tops, axis=0)
        total = jnp.sum(sums * jnp.exp(tops - top[None]), axis=0)
        own_top = to_lanes(colm[q])[0:1]
        colm[q] = to_rows(jnp.exp(own_top - top) / total)

        @pl.loop(0, 8)
        def _(i):
            rows = pl.ds(pl.multiple_of(i * 32, 32), 32)
            all_rows = pl.ds(pl.multiple_of(q * ROWS + i * 32, 32), 32)
            target = E[q, rows] * tile8(colm[q, rows])
            draft = dd[all_rows]
            chosen = columns == tile8(idc[all_rows])
            excess = jnp.maximum(target - draft, 0.0)
            E[q, rows] = excess
            cola[rows] = fold8(excess)
            colb[rows] = fold8(jnp.where(chosen, target, 0.0))
            colc[rows] = fold8(jnp.where(chosen, draft, 0.0))

        mass, picked, drafted = (
            jnp.sum(to_lanes(ref[...]), axis=0, keepdims=True) for ref in (cola, colb, colc)
        )
        token = jnp.concatenate([ids_ref[2 * q : 2 * q + 1], ids_ref[2 * q + 1 : 2 * q + 2]], axis=1)
        here = (token >= v * WIDTH) & (token < (v + 1) * WIDTH)
        ratio = jnp.where(here, jnp.minimum(1.0, picked / drafted), 0.0)
        S[q, 1, v, :, 0:ROWS] = mass
        S[q, 1, v, :, ROWS : 2 * ROWS] = ratio

    def finish(q):
        exchange_wait(q, 1)
        both = jnp.sum(S[q, 1], axis=0)
        acc_ref[q : q + 1] = both[:, ROWS : 2 * ROWS]
        colm[q] = to_rows(1.0 / jnp.maximum(both[:, 0:ROWS], mass_floor))

        @pl.loop(0, 8)
        def _(i):
            rows = pl.ds(pl.multiple_of(i * 32, 32), 32)
            E[q, rows] = E[q, rows] * tile8(colm[q, rows])

        cp = pltpu.make_async_copy(E.at[q], out_hbm.at[pl.ds(q * ROWS, ROWS)], loc.at[2 + q])
        cp.start()
        return cp

    spot = dr.at[pl.ds(pl.multiple_of(v * 8, 8), 8)]

    def draft_block(d):
        return dpk.at[:, pl.ds(pl.multiple_of(d * 768, 128), 768)]

    def draft_encode():
        draft_copy.wait()

        @pl.loop(0, 16)
        def _(i):
            block = dbuf[:, pl.ds(pl.multiple_of(i * 4096, 4096), 4096)]
            code = jnp.round(jnp.log(block) * -LOG_STEPS)
            code = jnp.minimum(jnp.maximum(code, 0.0), LOG_ZERO).astype(jnp.int32)
            words = [pack4(code[:, HALF * k : HALF * (k + 1)]) for k in range(8)]
            dpk[:, pl.ds(pl.multiple_of(i * 3072, 1024), 3072)] = jnp.concatenate(words, axis=1)

    def draft_send():
        pltpu.make_async_copy(draft_block(v), spot, dr_recv).start()

        @pl.loop(1, NV)
        def _(k):
            d = (v + k) % NV
            remote(draft_block(d), spot, dr_send, dr_recv, (r, d)).start()

    def draft_decode():
        pltpu.make_async_copy(dr, dr, dr_recv).wait()

        @pl.loop(0, 16)
        def _(i):
            rows = pl.ds(pl.multiple_of(i * 32, 32), 32)
            words = dr[rows]
            for k in range(2):
                w = words[:, PACKED * k : PACKED * (k + 1)]
                a, b, c = (w[:, 128 * j : 128 * (j + 1)] for j in range(3))
                d = (a & 255) | ((b & 255) << 8) | ((c & 255) << 16)
                for j, code in enumerate(((a >> 8) & 0xFFFFFF, (b >> 8) & 0xFFFFFF, (c >> 8) & 0xFFFFFF, d)):
                    code = code.astype(F32)
                    value = jnp.where(code < LOG_ZERO, jnp.exp(code * (-1.0 / LOG_STEPS)), 0.0)
                    dd[rows, HALF * k + 128 * j : HALF * k + 128 * (j + 1)] = value

    xf_x_start()
    zf_z(0)
    draft_encode()
    own_copy.wait()
    xf_x_end()
    xf_z(0)
    zf_z(1)
    zf_z(2)
    zf_x_end(0)
    sib(0)
    for j in range(4):
        idc[128 * j : 128 * j + 128] = to_rows(ids_ref[j : j + 1].astype(F32))
    zf_z(3)
    zf_z(4)
    w_copy.wait()
    sib_wait(0)
    product(0)
    for d in (1, 2, 3):
        a, b = 2 * d - 1, 2 * d
        xf_z(d)
        zf_x_end(a)
        sib(a)
        zf_x_end(b)
        sib(b)
        sib_wait(a)
        sib_wait(b)
        product(a)
        product(b)
    xf_z(4)
    zf_x_end(7)
    sib(7)
    sib_wait(7)
    product(7)
    draft_send()
    for nth in range(2):
        for side in range(2):
            onward(side, nth)
    draft_decode()
    fin_wait(0)
    local_stats(0)
    exchange(0, 0)
    fin_wait(1)
    local_stats(1)
    exchange(1, 0)
    local_excess(0)
    exchange(0, 1)
    local_excess(1)
    exchange(1, 1)
    out0 = finish(0)
    out1 = finish(1)

    for cp in sent:
        cp.wait_send()
    for j in range(8):
        product_sent(j)
    for q in range(2):
        for e in range(2):
            exchange_sent(q, e)
    some = dpk.at[:, pl.ds(0, (NV - 1) * 768)]
    remote(some, some, dr_send, dr_recv, to_sib).wait_send()
    out0.wait()
    out1.wait()


def local(hidden, head_weight, draft_probs, draft_ids):
    dma = pltpu.SemaphoreType.DMA
    residual, accept = pl.pallas_call(
        kernel,
        out_shape=(
            jax.ShapeDtypeStruct((2 * ROWS, WIDTH), F32),
            jax.ShapeDtypeStruct((2, ROWS), F32),
        ),
        in_specs=[pl.BlockSpec(memory_space=pltpu.HBM)] * 3 + [pl.BlockSpec(memory_space=pltpu.VMEM)],
        out_specs=(pl.BlockSpec(memory_space=pltpu.HBM), pl.BlockSpec(memory_space=pltpu.VMEM)),
        scratch_shapes=[
            pltpu.VMEM((NZ, NX, NC, SHARD, FEATURES), jnp.bfloat16),
            pltpu.VMEM((FEATURES, WIDTH), jnp.bfloat16),
            pltpu.VMEM((NZ, 2, ROWS, HALF), F32),
            pltpu.VMEM((2, 2, ROWS + 8, PACKED), jnp.int32),
            pltpu.VMEM((2, 2, 2, ROWS + 8, PACKED), jnp.int32),
            pltpu.VMEM((3, 2, 2, ROWS + 8, PACKED), jnp.int32),
            pltpu.VMEM((8, NV * WIDTH), F32),
            pltpu.VMEM((8, NV * 768), jnp.int32),
            pltpu.VMEM((2 * ROWS, 768), jnp.int32),
            pltpu.VMEM((2 * ROWS, WIDTH), F32),
            pltpu.VMEM((2, ROWS, WIDTH), F32),
            pltpu.VMEM((2 * ROWS, 128), F32),
            pltpu.VMEM((2, ROWS, 128), F32),
            pltpu.VMEM((ROWS, 128), F32),
            pltpu.VMEM((ROWS, 128), F32),
            pltpu.VMEM((ROWS, 128), F32),
            pltpu.VMEM((4, ROWS, 128), F32),
            pltpu.VMEM((2, 2, NV, 1, 2 * ROWS), F32),
            dma((AG_SEMS,)),
            dma((AG_SEMS,)),
            dma((20,)),
            dma((12,)),
            dma((2, 2)),
            dma((2, 2)),
            dma,
            dma,
            dma((5,)),
        ],
        compiler_params=pltpu.CompilerParams(
            collective_id=0, has_side_effects=True, vmem_limit_bytes=50 * 1024 * 1024
        ),
        cost_estimate=pl.CostEstimate(flops=7_516_192_768, bytes_accessed=16_000_000, transcendentals=524_288),
    )(hidden, head_weight, draft_probs, draft_ids.reshape(4, 128))
    return residual, accept.reshape(2 * ROWS)


def solution(mesh):
    in_specs = (P("vocab", "rows"), P("rows", "vocab"), P(("rows", "vocab"), None), P("rows", None))
    out_specs = (P("rows", "vocab"), P("rows"))
    return jax.shard_map(local, mesh=mesh, in_specs=in_specs, out_specs=out_specs, check_vma=False)
```

```python
import math

import jax
import jax.numpy as jnp
from jax import lax
from jax.experimental import pallas as pl
from jax.experimental.pallas import tpu as pltpu
from jax.sharding import PartitionSpec as P

MESH = pl.DeviceIdType.MESH
F32 = jnp.float32
mass_floor = 0.05

NY, NZ, NX, NC = 4, 8, 4, 2
NV = NZ * NX * NC
SHARD = 32
FEATURES = 1792
SPLIT = 1024
WIDTH = 1024
HALF = 512
ROWS = 256

ZF = pl.ds(0, SPLIT)
ZF_LO, ZF_HI = pl.ds(0, SPLIT // 2), pl.ds(SPLIT // 2, SPLIT // 2)
XF = pl.ds(SPLIT, FEATURES - SPLIT)
XF_LO = pl.ds(SPLIT, (FEATURES - SPLIT) // 2)
XF_HI = pl.ds((FEATURES + SPLIT) // 2, (FEATURES - SPLIT) // 2)

LEVELS = 8388600.0
STEPS = 64.0
PACKED = 384
LOG_STEPS = 2.0**17 / math.log(2.0)
LOG_ZERO = 2.0**24 - 1.0

ZZ, ZX, XX, XZ, SIB, AG_SEMS = 0, 8, 40, 44, 60, 68


def to_lanes(block):
    return jnp.transpose(block, (1, 0))


def to_rows(row):
    return jnp.transpose(jnp.broadcast_to(row, (128, row.shape[1])), (1, 0))


def tile8(block):
    return jnp.concatenate([block] * 8, axis=1)


def fold8(block):
    total = block[:, 0:128]
    for i in range(1, 8):
        total = total + block[:, 128 * i : 128 * (i + 1)]
    return total


def pack4(level):
    a, b, c, d = (level[:, 128 * k : 128 * (k + 1)] for k in range(4))
    words = ((a << 8) | (d & 255), (b << 8) | ((d >> 8) & 255), (c << 8) | ((d >> 16) & 255))
    return jnp.concatenate(words, axis=1)


def unpack(words, scale):
    a, b, c = (words[:, 128 * i : 128 * (i + 1)] for i in range(3))
    d = (a & 255) | ((b & 255) << 8) | ((c << 24) >> 8)
    return jnp.concatenate([q.astype(F32) * scale for q in (a >> 8, b >> 8, c >> 8, d)], axis=1)


def kernel(
    hid, w_hbm, draft_hbm, ids_ref, out_hbm, acc_ref, inv_ref,
    G, W, part, leg, fin, pk, dbuf, dpk, dr, dd, E, idc, colm, cola, colb, colc, colk, S,
    ag_send, ag_recv, y_send, y_recv, st_send, st_recv, dr_send, dr_recv, loc,
):
    r = lax.axis_index("rows")
    v = lax.axis_index("vocab")
    z = v // (NX * NC)
    x = (v // NC) % NX
    c = v % NC

    def vid(zz, xx, cc):
        return zz * (NX * NC) + xx * NC + cc

    def around(d):
        return (z + NZ + d) % NZ

    zp, zm = around(1), around(-1)
    xp, xm, xo = (x + 1) % NX, (x + NX - 1) % NX, (x + 2) % NX
    rp, rm = (r + 1) % NY, (r + NY - 1) % NY
    to_zp, to_zm = (r, vid(zp, x, c)), (r, vid(zm, x, c))
    to_zp2, to_zm2 = (r, vid(around(2), x, c)), (r, vid(around(-2), x, c))
    to_xp, to_xm, to_xo = (r, vid(z, xp, c)), (r, vid(z, xm, c)), (r, vid(z, xo, c))
    to_sib = (r, vid(z, x, 1 - c))
    order = [around(d) for d in (0, -1, 1, -2, 2, -3, 3, 4)]

    own_copy = pltpu.make_async_copy(hid, G.at[z, x, c], loc.at[0])
    own_copy.start()
    w_copy = pltpu.make_async_copy(w_hbm, W, loc.at[1])
    w_copy.start()
    draft_copy = pltpu.make_async_copy(draft_hbm, dbuf, loc.at[4])
    draft_copy.start()

    barrier = pltpu.get_barrier_semaphore()
    near = (to_zp, to_zm, to_zp2, to_zm2, to_xp, to_xm, to_xo, to_sib, (rp, v), (rm, v))
    for dev in near:
        pl.semaphore_signal(barrier, inc=1, device_id=dev, device_id_type=MESH)
    pl.semaphore_wait(barrier, len(near))

    sent = []

    def remote(src, dst, ss, rs, dev):
        return pltpu.make_async_remote_copy(
            src_ref=src, dst_ref=dst, send_sem=ss, recv_sem=rs, device_id=dev, device_id_type=MESH
        )

    def wait_recv(region, rs):
        remote(region, region, rs, rs, to_sib).wait_recv()

    def spread(region, sem, dev, src=None):
        cp = remote(region if src is None else src, region, ag_send.at[sem], ag_recv.at[sem], dev)
        cp.start()
        sent.append(cp)

    def arrived(region, sem):
        wait_recv(region, ag_recv.at[sem])

    def zf(zz, xx, cols=ZF):
        return G.at[zz, xx, c, :, cols]

    def zf_x_send(j):
        src = hid.at[:, ZF] if j == 0 else None
        for k, dev in enumerate((to_xp, to_xm, to_xo)):
            spread(zf(order[j], x), ZX + 4 * j + k, dev, src)

    def zf_x_end(j):
        for k, xx in enumerate((xm, xp, xo)):
            arrived(zf(order[j], xx), ZX + 4 * j + k)

    def zf_z(d):
        if d == 0:
            for k, dev in enumerate((to_zp, to_zm, to_zp2, to_zm2)):
                spread(zf(z, x), ZZ + k, dev, hid.at[:, ZF])
            zf_x_send(0)
            return
        if d == 4:
            arrived(zf(order[7], x, ZF_LO), ZZ + 6)
            arrived(zf(order[7], x, ZF_HI), ZZ + 7)
            zf_x_send(7)
            return
        za, zb = order[2 * d - 1], order[2 * d]
        arrived(zf(za, x), ZZ + 2 * d - 2)
        if d == 2:
            spread(zf(za, x), ZZ + 4, to_zp)
            spread(zf(za, x, ZF_LO), ZZ + 6, to_zp2)
        zf_x_send(2 * d - 1)
        arrived(zf(zb, x), ZZ + 2 * d - 1)
        if d == 2:
            spread(zf(zb, x), ZZ + 5, to_zm)
            spread(zf(zb, x, ZF_HI), ZZ + 7, to_zm2)
        zf_x_send(2 * d)

    def xf(xx, cols=XF):
        return G.at[z, xx, c, :, cols]

    def xfs(zz, cols=XF):
        return G.at[zz, :, c, :, cols]

    def xf_x_start():
        spread(xf(x), XX, to_xp, hid.at[:, XF])
        spread(xf(x), XX + 1, to_xm, hid.at[:, XF])
        spread(xf(x), XX + 2, to_xo, hid.at[:, XF])

    def xf_x_end():
        arrived(xf(xm), XX)
        arrived(xf(xp), XX + 1)
        arrived(xf(xo), XX + 2)

    def xf_z(d):
        if d == 0:
            spread(xfs(z, XF_LO), XZ, to_zp)
            spread(xfs(z, XF_HI), XZ + 3, to_zm)
            spread(xfs(z, XF_HI), XZ + 1, to_zp)
            spread(xfs(z, XF_LO), XZ + 2, to_zm)
            return
        if d == 4:
            arrived(xfs(order[7], XF_LO), XZ + 12)
            arrived(xfs(order[7], XF_HI), XZ + 13)
            return
        za, zb = order[2 * d - 1], order[2 * d]
        o = XZ + 4 * d
        arrived(xfs(za, XF_LO), o - 4)
        spread(xfs(za, XF_LO), o, to_zp)
        arrived(xfs(zb, XF_HI), o - 1)
        spread(xfs(zb, XF_HI), o + (1 if d == 3 else 3), to_zm)
        arrived(xfs(za, XF_HI), o - 3)
        arrived(xfs(zb, XF_LO), o - 2)
        if d < 3:
            spread(xfs(za, XF_HI), o + 1, to_zp)
            spread(xfs(zb, XF_LO), o + 2, to_zm)

    def sib(j):
        spread(G.at[order[j], :, c], SIB + j, to_sib)

    def sib_wait(j):
        arrived(G.at[order[j], :, 1 - c], SIB + j)

    def role(zz):
        return (zz // 2 - r + NY) % NY, zz % 2

    odd = z % 2
    far_down = (role(around(-2))[0] == 2).astype(jnp.int32)
    far_up = (role(around(2))[0] == 2).astype(jnp.int32)
    work = [z]
    for d in (1, 2, 3):
        up = odd if d != 2 else odd * far_up + (1 - odd) * (1 - far_down)
        work += [around(d * (2 * up - 1)), around(-d * (2 * up - 1))]
    work.append(order[7])

    def far_left(q, j):
        return remote(pk.at[0, q, 0], leg.at[0, q], y_send.at[2 * j], y_recv.at[q], (rp, v))

    def far_right(q, j):
        return remote(pk.at[0, q, 1], leg.at[1, q], y_send.at[2 * j + 1], y_recv.at[2 + q], (rm, v))

    def near_right(q, j):
        return remote(pk.at[1, q, 1], fin.at[q, 0, 1], y_send.at[2 * j + 1], y_recv.at[4 + q], (rp, v))

    def near_left(q, j):
        return remote(pk.at[1, q, 0], fin.at[q, 1, 0], y_send.at[2 * j], y_recv.at[6 + q], (rm, v))

    def pack(zz, side, dst):
        @pl.loop(0, 4)
        def _(i):
            rows = pl.ds(pl.multiple_of(i * 64, 64), 64)
            block = part[zz, side, rows]
            unit = jnp.floor(jnp.max(jnp.abs(block), axis=1, keepdims=True) * STEPS) + 1.0
            colk[0, rows] = jnp.broadcast_to(unit, (64, 128))
            level = jnp.round(block * (LEVELS * STEPS / unit)).astype(jnp.int32)
            dst[rows] = pack4(level)

        dst[ROWS : ROWS + 1, 0:ROWS] = to_lanes(colk[0])[0:1].astype(jnp.int32)

    def scales(src, k):
        colk[k] = to_rows(src[ROWS : ROWS + 1, 0:ROWS].astype(F32)) * (1.0 / (LEVELS * STEPS))

    def product(j):
        zz = work[j]

        lhs = G[zz].reshape(ROWS, FEATURES)
        for n in range(2):
            part[zz, n] = jnp.dot(lhs, W[:, HALF * n : HALF * (n + 1)], preferred_element_type=F32)

        d, q = role(zz)

        @pl.when(d == 2)
        def _():
            pack(zz, 0, pk.at[0, q, 0])
            far_left(q, j).start()
            pack(zz, 1, pk.at[0, q, 1])
            far_right(q, j).start()

        @pl.when(d == 1)
        def _():
            pack(zz, 1, pk.at[1, q, 1])
            near_right(q, j).start()

        @pl.when(d == 3)
        def _():
            pack(zz, 0, pk.at[1, q, 0])
            near_left(q, j).start()

    def product_sent(j):
        d, q = role(work[j])

        @pl.when(d >= 2)
        def _():
            far_left(q, j).wait_send()

        @pl.when((d == 1) | (d == 2))
        def _():
            far_right(q, j).wait_send()

    def add_leg(zz, side, q):
        scales(leg.at[side, q], 1)

        @pl.loop(0, 4)
        def _(i):
            rows = pl.ds(pl.multiple_of(i * 64, 64), 64)
            part[zz, side, rows] = part[zz, side, rows] + unpack(leg[side, q, rows], colk[1, rows])

    def steps_to(zz):
        up, down = (zz - z + NZ) % NZ, (z - zz + NZ) % NZ
        return jnp.minimum(up, down)

    def onward(side, nth):
        owner = (rp, rm)[side]
        second = (steps_to(2 * owner + 1) < steps_to(2 * owner)).astype(jnp.int32)
        q = second if nth == 0 else 1 - second
        zz = 2 * owner + q
        wait_recv(leg.at[side, q], y_recv.at[2 * side + q])
        add_leg(zz, side, q)
        pack(zz, side, pk.at[2, q, side])
        cp = remote(
            pk.at[2, q, side], fin.at[q, side, side], y_send.at[16 + 2 * side + q],
            y_recv.at[8 + 2 * side + q], (owner, v),
        )
        cp.start()
        sent.append(cp)

    def fin_wait(q):
        wait_recv(fin.at[q, 0, 1], y_recv.at[4 + q])
        wait_recv(fin.at[q, 1, 0], y_recv.at[6 + q])
        wait_recv(fin.at[q, 0, 0], y_recv.at[8 + q])
        wait_recv(fin.at[q, 1, 1], y_recv.at[10 + q])

    def exchange(q, e):
        mine = S.at[q, e, v]

        @pl.loop(0, NZ, unroll=True)
        def _(i):
            dz = 4 + (1 - 2 * (i % 2)) * ((i + 1) // 2)
            zz = (z + dz) % NZ
            for dx in (2, 1, 3, 0):
                for dc in (1, 0):
                    cp = remote(
                        mine, mine, st_send.at[q, e], st_recv.at[q, e],
                        (r, vid(zz, (x + dx) % NX, (c + dc) % NC)),
                    )
                    if dx == 0 and dc == 0:
                        pl.when(i < NZ - 1)(cp.start)
                    else:
                        cp.start()

    def exchange_wait(q, e):
        wait_recv(S.at[q, e, pl.ds(0, NV - 1)], st_recv.at[q, e])

    def exchange_sent(q, e):
        region = S.at[q, e, pl.ds(0, NV - 1)]
        remote(region, region, st_send.at[q, e], st_recv.at[q, e], to_sib).wait_send()

    def local_stats(q):
        zz = 2 * r + q
        for side in range(2):
            for k in range(2):
                scales(fin.at[q, k, side], 2 * side + k)

        @pl.loop(0, 8)
        def _(i):
            rows = pl.ds(pl.multiple_of(i * 32, 32), 32)
            halves = []
            for side in range(2):
                below = unpack(fin[q, 0, side, rows], colk[2 * side, rows])
                above = unpack(fin[q, 1, side, rows], colk[2 * side + 1, rows])
                halves.append(part[zz, side, rows] + (below + above))
            logit = jnp.concatenate(halves, axis=1)
            top = jnp.max(logit, axis=1, keepdims=True)
            weight = jnp.exp(logit - top)
            E[q, rows] = weight
            colm[q, rows] = jnp.broadcast_to(top, (32, 128))
            cola[rows] = fold8(weight)

        S[q, 0, v, :, 0:ROWS] = to_lanes(colm[q])[0:1]
        S[q, 0, v, :, ROWS : 2 * ROWS] = jnp.sum(to_lanes(cola[...]), axis=0, keepdims=True)

    columns = (lax.broadcasted_iota(jnp.int32, (32, WIDTH), 1) + v * WIDTH).astype(F32)

    def local_excess(q):
        exchange_wait(q, 0)
        tops = S[q, 0, :, :, 0:ROWS]
        sums = S[q, 0, :, :, ROWS : 2 * ROWS]
        top = jnp.max(tops, axis=0)
        total = jnp.sum(sums * jnp.exp(tops - top[None]), axis=0)
        own_top = to_lanes(colm[q])[0:1]
        colm[q] = to_rows(jnp.exp(own_top - top) / total)

        @pl.loop(0, 8)
        def _(i):
            rows = pl.ds(pl.multiple_of(i * 32, 32), 32)
            all_rows = pl.ds(pl.multiple_of(q * ROWS + i * 32, 32), 32)
            target = E[q, rows] * tile8(colm[q, rows])
            draft = dd[all_rows]
            chosen = columns == tile8(idc[all_rows])
            excess = jnp.maximum(target - draft, 0.0)
            E[q, rows] = excess
            cola[rows] = fold8(excess)
            colb[rows] = fold8(jnp.where(chosen, target, 0.0))
            colc[rows] = fold8(jnp.where(chosen, draft, 0.0))

        mass, picked, drafted = (
            jnp.sum(to_lanes(ref[...]), axis=0, keepdims=True) for ref in (cola, colb, colc)
        )
        token = jnp.concatenate([ids_ref[2 * q : 2 * q + 1], ids_ref[2 * q + 1 : 2 * q + 2]], axis=1)
        here = (token >= v * WIDTH) & (token < (v + 1) * WIDTH)
        ratio = jnp.where(here, jnp.minimum(1.0, picked / drafted), 0.0)
        S[q, 1, v, :, 0:ROWS] = mass
        S[q, 1, v, :, ROWS : 2 * ROWS] = ratio

    def finish(q):
        exchange_wait(q, 1)
        both = jnp.sum(S[q, 1], axis=0)
        acc_ref[q : q + 1] = both[:, ROWS : 2 * ROWS]
        inv_ref[q : q + 1] = 1.0 / jnp.maximum(both[:, 0:ROWS], mass_floor)

    def leave(q):
        cp = pltpu.make_async_copy(E.at[q], out_hbm.at[pl.ds(q * ROWS, ROWS)], loc.at[2 + q])
        cp.start()
        return cp

    spot = dr.at[pl.ds(pl.multiple_of(v * 8, 8), 8)]

    def draft_block(d):
        return dpk.at[:, pl.ds(pl.multiple_of(d * 768, 128), 768)]

    def draft_encode():
        draft_copy.wait()

        @pl.loop(0, 16)
        def _(i):
            block = dbuf[:, pl.ds(pl.multiple_of(i * 4096, 4096), 4096)]
            code = jnp.round(jnp.log(block) * -LOG_STEPS)
            code = jnp.minimum(jnp.maximum(code, 0.0), LOG_ZERO).astype(jnp.int32)
            words = [pack4(code[:, HALF * k : HALF * (k + 1)]) for k in range(8)]
            dpk[:, pl.ds(pl.multiple_of(i * 3072, 1024), 3072)] = jnp.concatenate(words, axis=1)

    def draft_send():
        pltpu.make_async_copy(draft_block(v), spot, dr_recv).start()

        @pl.loop(1, NV, unroll=7)
        def _(k):
            d = (v + k) % NV
            remote(draft_block(d), spot, dr_send, dr_recv, (r, d)).start()

    def draft_decode():
        pltpu.make_async_copy(dr, dr, dr_recv).wait()

        @pl.loop(0, 16)
        def _(i):
            rows = pl.ds(pl.multiple_of(i * 32, 32), 32)
            words = dr[rows]
            for k in range(2):
                w = words[:, PACKED * k : PACKED * (k + 1)]
                a, b, c = (w[:, 128 * j : 128 * (j + 1)] for j in range(3))
                d = (a & 255) | ((b & 255) << 8) | ((c & 255) << 16)
                for j, code in enumerate(((a >> 8) & 0xFFFFFF, (b >> 8) & 0xFFFFFF, (c >> 8) & 0xFFFFFF, d)):
                    code = code.astype(F32)
                    value = jnp.where(code < LOG_ZERO, jnp.exp(code * (-1.0 / LOG_STEPS)), 0.0)
                    dd[rows, HALF * k + 128 * j : HALF * k + 128 * (j + 1)] = value

    xf_x_start()
    zf_z(0)
    draft_encode()
    own_copy.wait()
    xf_x_end()
    xf_z(0)
    zf_z(1)
    zf_z(2)
    zf_x_end(0)
    sib(0)
    for j in range(4):
        idc[128 * j : 128 * j + 128] = to_rows(ids_ref[j : j + 1].astype(F32))
    zf_z(3)
    zf_z(4)
    w_copy.wait()
    sib_wait(0)
    product(0)
    for d in (1, 2, 3):
        a, b = 2 * d - 1, 2 * d
        xf_z(d)
        zf_x_end(a)
        sib(a)
        zf_x_end(b)
        sib(b)
        sib_wait(a)
        sib_wait(b)
        product(a)
        product(b)
    xf_z(4)
    zf_x_end(7)
    sib(7)
    sib_wait(7)
    product(7)
    draft_send()
    for nth in range(2):
        for side in range(2):
            onward(side, nth)
    fin_wait(0)
    local_stats(0)
    exchange(0, 0)
    fin_wait(1)
    local_stats(1)
    exchange(1, 0)
    draft_decode()
    local_excess(0)
    exchange(0, 1)
    local_excess(1)
    exchange(1, 1)
    out0 = leave(0)
    out1 = leave(1)
    finish(0)
    finish(1)

    for cp in sent:
        cp.wait_send()
    for j in range(8):
        product_sent(j)
    for q in range(2):
        for e in range(2):
            exchange_sent(q, e)
    some = dpk.at[:, pl.ds(0, (NV - 1) * 768)]
    remote(some, some, dr_send, dr_recv, to_sib).wait_send()
    out0.wait()
    out1.wait()


def local(hidden, head_weight, draft_probs, draft_ids):
    dma = pltpu.SemaphoreType.DMA
    excess, accept, inverse = pl.pallas_call(
        kernel,
        out_shape=(
            jax.ShapeDtypeStruct((2 * ROWS, WIDTH), F32),
            jax.ShapeDtypeStruct((2, ROWS), F32),
            jax.ShapeDtypeStruct((2, ROWS), F32),
        ),
        in_specs=[pl.BlockSpec(memory_space=pltpu.HBM)] * 3 + [pl.BlockSpec(memory_space=pltpu.VMEM)],
        out_specs=(pl.BlockSpec(memory_space=pltpu.HBM),) + (pl.BlockSpec(memory_space=pltpu.VMEM),) * 2,
        scratch_shapes=[
            pltpu.VMEM((NZ, NX, NC, SHARD, FEATURES), jnp.bfloat16),
            pltpu.VMEM((FEATURES, WIDTH), jnp.bfloat16),
            pltpu.VMEM((NZ, 2, ROWS, HALF), F32),
            pltpu.VMEM((2, 2, ROWS + 8, PACKED), jnp.int32),
            pltpu.VMEM((2, 2, 2, ROWS + 8, PACKED), jnp.int32),
            pltpu.VMEM((3, 2, 2, ROWS + 8, PACKED), jnp.int32),
            pltpu.VMEM((8, NV * WIDTH), F32),
            pltpu.VMEM((8, NV * 768), jnp.int32),
            pltpu.VMEM((2 * ROWS, 768), jnp.int32),
            pltpu.VMEM((2 * ROWS, WIDTH), F32),
            pltpu.VMEM((2, ROWS, WIDTH), F32),
            pltpu.VMEM((2 * ROWS, 128), F32),
            pltpu.VMEM((2, ROWS, 128), F32),
            pltpu.VMEM((ROWS, 128), F32),
            pltpu.VMEM((ROWS, 128), F32),
            pltpu.VMEM((ROWS, 128), F32),
            pltpu.VMEM((4, ROWS, 128), F32),
            pltpu.VMEM((2, 2, NV, 1, 2 * ROWS), F32),
            dma((AG_SEMS,)),
            dma((AG_SEMS,)),
            dma((20,)),
            dma((12,)),
            dma((2, 2)),
            dma((2, 2)),
            dma,
            dma,
            dma((5,)),
        ],
        compiler_params=pltpu.CompilerParams(
            collective_id=0, has_side_effects=True, vmem_limit_bytes=50 * 1024 * 1024
        ),
        cost_estimate=pl.CostEstimate(flops=7_516_192_768, bytes_accessed=16_000_000, transcendentals=524_288),
    )(hidden, head_weight, draft_probs, draft_ids.reshape(4, 128))
    return excess * inverse.reshape(2 * ROWS, 1), accept.reshape(2 * ROWS)


def solution(mesh):
    in_specs = (P("vocab", "rows"), P("rows", "vocab"), P(("rows", "vocab"), None), P("rows", None))
    out_specs = (P("rows", "vocab"), P("rows"))
    return jax.shard_map(local, mesh=mesh, in_specs=in_specs, out_specs=out_specs, check_vma=False)
```
